128 devices in a mesh: gx: 4 (over x), gy: 32 (over z, y, core).
Axes of the slice: x: 4, y: 4, z: 4, core: 2. Of those that a mesh axis runs over, the one named last changes fastest.
Arguments:
- right_side: float32 [8, 3, 64, 4096], P(None, None, 'gx', 'gy'), may hold values from -50 to 50
- first_guess: float32 [8, 3, 64, 4096], P(None, None, 'gx', 'gy'), may hold values from -3 to 3
- diag_block: bfloat16 [8, 3, 3, 64, 4096], P(None, None, None, 'gx', 'gy'), may hold values from -2.41 to 12
- mobility: bfloat16 [8, 3, 3, 64, 4096], P(None, None, None, 'gx', 'gy'), may hold values from -1 to 1.21
- face_trans: bfloat16 [6, 8, 64, 4096], P(None, None, 'gx', 'gy'), may hold values from 0.19921875 to 1
- column_inverse: bfloat16 [4, 6, 6, 64, 4096], P(None, None, None, 'gx', 'gy'), may hold values from -0.061 to 0.201
- perf_cell: int32 [128, 128, 10], P(('gx', 'gy')), may hold values from 0 to 16383, as said below
- perf_slot: int32 [128, 128, 10], P(('gx', 'gy')), may hold values from 0 to 1024, as said below
- well_in: float32 [3, 131072], P(None, ('gx', 'gy')), may hold values from -4 to 4
- well_out: float32 [3, 131072], P(None, ('gx', 'gy')), may hold values from -4 to 4
- well_inverse: float32 [1024, 128, 128], P(('gx', 'gy')), may hold values from -1 to 1
Outputs:
- solution: float32 [8, 3, 64, 4096], P(None, None, 'gx', 'gy')
- residual: float32 [8, 3, 64, 4096], P(None, None, 'gx', 'gy')
The draws below stay inside these ranges and needn't reach their ends.
Inputs may be any that keep to these rules, and one draw needn't show every extreme that they name: `perf_cell`: entry [s, d, q] is a local cell number of device s's tile, the cell of slot q from device s to owner d; the slot's segment is perf_slot[d, s, q]; slots that perf_slot marks empty carry an arbitrary cell. `perf_slot`: entry [d, s, q] is w * 128 + g when slot q from device s carries segment g of owner d's local well w, and 1024 when the slot is empty. Each segment of an owner appears at most once; the segments of a well that appear are 0 to n - 1 for its padded count n of 1 to 128. Every pair (d, s) has at most 10 live slots and some pair has exactly 10; in every draw some owner has all 1024 segments live.
All inputs are finite; a program needn't handle non-finite values.
Results may differ from the reference program's by a relative error of at most 0.0003.
Values sent between devices are 32-bit elements; how exact they have to be, the bound alone decides.
A program may use at most 128 MiB of HBM per device.

```python
import math
import jax
import jax.numpy as jnp
from jax import lax

CX = 16
CY = 128
NZ = 8
W_DEV = 8
SEG = 128
ITERS = 2
NX = 64
NY = 4096
WELLS = 1024
CAP = 10
N_GY = 32
DEVICES = 128


def block_matrix(key, full_shape, row_dim, col_dim, low_diag, high_diag, off_scale):
    subkeys = jax.random.split(key, 2)
    row_pos = lax.broadcasted_iota(jnp.int32, full_shape, row_dim)
    col_pos = lax.broadcasted_iota(jnp.int32, full_shape, col_dim)
    leading = jnp.exp(jax.random.uniform(subkeys[0], full_shape, jnp.float32, math.log(low_diag), math.log(high_diag)))
    spread = jnp.clip(jax.random.normal(subkeys[1], full_shape, jnp.float32), -3.0, 3.0) * off_scale
    return jnp.where(row_pos == col_pos, leading, spread)


def draw_right_side(key, part):
    subkeys = jax.random.split(key, 2)
    full_shape = (NZ, 3, NX, NY)
    second_pos = lax.broadcasted_iota(jnp.float32, full_shape, 3) / max(NY - 1, 1)
    cell_scale = jnp.exp(jax.random.uniform(subkeys[1], full_shape, jnp.float32, math.log(0.3), math.log(3.0)))
    ramp_second = 1.0 + 2.0 * second_pos
    rough = jnp.clip(jax.random.normal(subkeys[0], full_shape, jnp.float32), -4.0, 4.0)
    return rough * cell_scale * ramp_second


def draw_diag_block(key, part):
    return block_matrix(key, (NZ, 3, 3, NX, NY), 1, 2, 6.0, 12.0, 0.8).astype(jnp.bfloat16)


def draw_mobility(key, part):
    return block_matrix(key, (NZ, 3, 3, NX, NY), 1, 2, 0.5, 1.2, 0.25).astype(jnp.bfloat16)


def draw_column_inverse(key, part):
    return block_matrix(key, (NZ // 2, 6, 6, NX, NY), 1, 2, 0.08, 0.2, 0.02).astype(jnp.bfloat16)


def draw_well_inverse(key, part):
    return block_matrix(key, (WELLS, SEG, SEG), 1, 2, 0.3, 1.0, 0.3 / math.sqrt(SEG))


def perforation_tables(key):
    subkeys = jax.random.split(jax.random.fold_in(key, 17), 6)
    slot_total = DEVICES * CAP
    longest = jax.random.randint(subkeys[0], (DEVICES, 1), max(SEG // 4, 1), SEG + 1)
    shortest = jnp.maximum(longest // 2, 1)
    counts = jax.random.randint(subkeys[1], (DEVICES, W_DEV), shortest, longest + 1)
    heavy_owner = jax.random.randint(subkeys[2], (), 0, DEVICES)
    owners = jnp.arange(DEVICES, dtype=jnp.int32)[:, None]
    counts = jnp.where(owners == heavy_owner, SEG, counts).astype(jnp.int32)
    seg_ends = jnp.cumsum(counts, axis=1).astype(jnp.int32)
    starts = seg_ends - counts
    live_total = seg_ends[:, -1:]
    forced = jax.random.randint(subkeys[3], (DEVICES, 1), 0, DEVICES)
    position = jnp.arange(slot_total, dtype=jnp.int32)[None, :]
    scores = jax.random.randint(subkeys[4], (DEVICES, slot_total), 1, 1024) * slot_total + position
    scores = jnp.where(position // CAP == forced, position, scores)
    sorted_order = jnp.argsort(scores, axis=1, stable=True)
    slot_rank = jnp.argsort(sorted_order, axis=1, stable=True).astype(jnp.int32)
    well_of = jnp.sum((seg_ends[:, None, :] <= slot_rank[:, :, None]).astype(jnp.int32), axis=2)
    well_of = jnp.minimum(well_of, W_DEV - 1)
    segment = slot_rank - jnp.take_along_axis(starts, well_of, axis=1)
    target = jnp.where(slot_rank < live_total, well_of * SEG + segment, W_DEV * SEG).astype(jnp.int32)
    cell_ids = jax.random.randint(subkeys[5], (DEVICES, slot_total), 0, NZ * CX * CY).astype(jnp.int32)
    return (target.reshape(DEVICES, DEVICES, CAP), cell_ids.reshape(DEVICES, DEVICES, CAP))


def draw_perf_cell(key, part):
    target, cell_ids = perforation_tables(key)
    return jnp.transpose(cell_ids, (1, 0, 2))


def draw_perf_slot(key, part):
    target, cell_ids = perforation_tables(key)
    return target


def level_of(own_key, shape, cuts, low, top_value):
    level = 1.0
    for dim, shards_of in cuts:
        heights = jax.random.uniform(jax.random.fold_in(jax.random.fold_in(own_key, 6), dim), (shards_of,), jnp.float32, low / len(cuts), top_value / len(cuts))
        level = level * jnp.repeat(jnp.exp(heights), shape[dim] // shards_of).reshape((-1,) + (1,) * (len(shape) - 1 - dim))
    return level


def normal_values(stream_key, dims, scale, reach, cuts=(), held_as=jnp.bfloat16):
    level = level_of(stream_key, dims, cuts, -0.22, 0.18) if cuts else 1.0
    entries = jax.random.normal(stream_key, dims, jnp.float32) * scale * level
    return jnp.minimum(jnp.maximum(entries, -reach), reach).astype(held_as)


def setup_inputs(seed: int = 0) -> dict:
    key_list = jax.random.split(jax.random.key(seed), 12)
    right_side = draw_right_side(jax.random.fold_in(key_list[11], 71), 0)
    first_guess = normal_values(key_list[1], (NZ, 3, NX, NY), 0.5, 3.0, ((2, 4), (3, 32)), jnp.float32)
    diag_block = draw_diag_block(jax.random.fold_in(key_list[11], 71), 0)
    mobility = draw_mobility(jax.random.fold_in(key_list[11], 71), 0)
    face_trans = jnp.clip(0.19921875 + 0.80078125 * jax.random.uniform(key_list[4], (6, NZ, NX, NY), jnp.float32) ** level_of(key_list[4], (6, NZ, NX, NY), ((2, 4), (3, 32)), -0.2, 0.2), 0.19921875, 1.0).astype(jnp.bfloat16)
    column_inverse = draw_column_inverse(jax.random.fold_in(key_list[11], 71), 0)
    perf_cell = draw_perf_cell(jax.random.fold_in(key_list[11], 71), 0)
    perf_slot = draw_perf_slot(jax.random.fold_in(key_list[11], 71), 0)
    well_in = normal_values(key_list[8], (3, WELLS * SEG), 0.7, 4.0, ((1, 128),), jnp.float32)
    well_out = normal_values(key_list[9], (3, WELLS * SEG), 0.7, 4.0, ((1, 128),), jnp.float32)
    well_inverse = draw_well_inverse(jax.random.fold_in(key_list[11], 71), 0)
    return {"right_side": right_side, "first_guess": first_guess, "diag_block": diag_block, "mobility": mobility, "face_trans": face_trans, "column_inverse": column_inverse, "perf_cell": perf_cell, "perf_slot": perf_slot, "well_in": well_in, "well_out": well_out, "well_inverse": well_inverse}


def couple(mixing, vector):
    summed = mixing[:, :, 0].astype(jnp.float32) * vector[:, 0:1]
    summed = summed + mixing[:, :, 1].astype(jnp.float32) * vector[:, 1:2]
    summed = summed + mixing[:, :, 2].astype(jnp.float32) * vector[:, 2:3]
    return summed


def stencil(vector, extended, diag_block, face_trans):
    factor = face_trans.astype(jnp.float32)[:, :, None]
    interior = extended[:, :, 1:-1, 1:-1]
    zero_layer = jnp.zeros_like(interior[:1])
    under_layer = jnp.concatenate([zero_layer, interior[:-1]], axis=0)
    over_layer = jnp.concatenate([interior[1:], zero_layer], axis=0)
    beside = factor[0] * extended[:, :, :-2, 1:-1]
    beside = beside + factor[1] * extended[:, :, 2:, 1:-1]
    beside = beside + factor[2] * extended[:, :, 1:-1, :-2]
    beside = beside + factor[3] * extended[:, :, 1:-1, 2:]
    beside = beside + factor[4] * under_layer
    beside = beside + factor[5] * over_layer
    return couple(diag_block, vector) - beside


def precondition(vector, column_inverse):
    layers, comps, tile_rows, tile_cols = vector.shape
    paired = vector.reshape(layers // 2, 6, tile_rows, tile_cols)
    result = column_inverse[:, :, 0].astype(jnp.float32) * paired[:, 0:1]
    for member in range(1, 6):
        result = result + column_inverse[:, :, member].astype(jnp.float32) * paired[:, member:member + 1]
    return result.reshape(vector.shape)


def well_term(vector, perf_cell, perf_slot, well_in, well_out, well_inverse):
    source = jnp.arange(DEVICES, dtype=jnp.int32)[:, None, None]
    owner_id = jnp.arange(DEVICES, dtype=jnp.int32)[None, :, None]
    layer_idx = perf_cell // (CX * CY)
    in_tile = perf_cell % (CX * CY)
    first_idx = (source // N_GY) * CX + in_tile // CY
    second_idx = (source % N_GY) * CY + in_tile % CY
    values = vector[layer_idx, :, first_idx, second_idx]
    local_slot = jnp.transpose(perf_slot, (1, 0, 2))
    per_owner = W_DEV * SEG
    target = jnp.where(local_slot < per_owner, owner_id * per_owner + local_slot, WELLS * SEG).astype(jnp.int32)
    pad_in = jnp.concatenate([well_in, jnp.zeros((3, 1), jnp.float32)], axis=1)
    pad_out = jnp.concatenate([well_out, jnp.zeros((3, 1), jnp.float32)], axis=1)
    rate = pad_in[0][target] * values[..., 0] + pad_in[1][target] * values[..., 1] + pad_in[2][target] * values[..., 2]
    totals = jnp.zeros((WELLS * SEG + 1,), jnp.float32).at[target].add(rate)
    seg_rate = jnp.einsum("wgh,wh->wg", well_inverse.astype(jnp.float32), totals[:WELLS * SEG].reshape(WELLS, SEG), precision=lax.Precision.HIGHEST)
    padded = jnp.concatenate([seg_rate.reshape(-1), jnp.zeros((1,), jnp.float32)])
    back = padded[target]
    terms = jnp.stack([pad_out[0][target] * back, pad_out[1][target] * back, pad_out[2][target] * back], axis=-1)
    return jnp.zeros_like(vector).at[layer_idx, :, first_idx, second_idx].add(terms)


def reference(right_side, first_guess, diag_block, mobility, face_trans, column_inverse, perf_cell, perf_slot, well_in, well_out, well_inverse):
    def apply_operator(vector):
        flux = couple(mobility, vector)
        extended = jnp.pad(flux, ((0, 0), (0, 0), (1, 1), (1, 1)))
        return stencil(vector, extended, diag_block, face_trans) - well_term(vector, perf_cell, perf_slot, well_in, well_out, well_inverse)

    iterate = first_guess
    residual = right_side - apply_operator(iterate)
    shadow = residual
    inner_now = jnp.sum(shadow * residual)
    search = residual
    for iteration in range(ITERS):
        search_hat = precondition(search, column_inverse)
        applied = apply_operator(search_hat)
        projected = jnp.sum(shadow * applied)
        step_size = inner_now / projected
        halfway = residual - step_size * applied
        halfway_hat = precondition(halfway, column_inverse)
        response = apply_operator(halfway_hat)
        smoothing = jnp.sum(response * halfway) / jnp.sum(response * response)
        iterate = iterate + step_size * search_hat + smoothing * halfway_hat
        residual = halfway - smoothing * response
        if iteration + 1 < ITERS:
            inner_next = jnp.sum(shadow * residual)
            momentum = (inner_next / inner_now) * (step_size / smoothing)
            search = residual + momentum * (search - smoothing * applied)
            inner_now = inner_next
    return iterate, right_side - apply_operator(iterate)
```

```python
import jax
import jax.numpy as jnp
from jax import lax
from jax.experimental import pallas as pl
from jax.experimental.pallas import tpu as pltpu
from jax.sharding import PartitionSpec as P

MESH = pl.DeviceIdType.MESH
F32 = jnp.float32
BF16 = jnp.bfloat16
DEV = 128
CAP = 10
SLOTS = DEV * CAP
OPS = 5
EXCHANGES = 2 * OPS + 1


def dot(a, b):
    return lax.dot_general(a, b, (((1,), (0,)), ((), ())), preferred_element_type=F32)


def dot_nt(a, b):
    return lax.dot_general(a, b, (((1,), (1,)), ((), ())), preferred_element_type=F32)


def split(value):
    high = value.astype(BF16).astype(F32)
    return high, value - high


def flat(value):
    return value.reshape(128, 128)


def local_sum(lefts, rights):
    total = lefts[0] * rights[0] + lefts[1] * rights[1] + lefts[2] * rights[2]
    return jnp.sum(jnp.sum(total, axis=0, keepdims=True), axis=1, keepdims=True)


def kernel(
    right_ref, guess_ref, diag_ref, mob_ref, face_ref, colinv_ref, cell_ref, slot_ref, win_ref,
    wout_ref, winv_ref, sol_ref, res_ref,
    snd, rcv, flux_pad, col_snd, col_rcv, mt, pads, faces, oht, cmt, gts, gt, wmask, w2, vals, coef,
    snd_sem, rcv_sem, hs_sem, hr_sem,
):
    gx = lax.axis_index("gx")
    gy = lax.axis_index("gy")
    me = gx * 32 + gy
    pz, py, pc = gy // 8, (gy // 2) % 4, gy % 2

    def peer(i):
        tx, tz, ty = 3 - i // 32, 3 - (i // 8) % 4, 3 - (i // 2) % 4
        ox, oz, oy = (tx * (tx + 1) // 2) % 4, (tz * (tz + 1) // 2) % 4, (ty * (ty + 1) // 2) % 4
        oc = 1 - i % 2
        return (gx + ox) % 4, ((pz + oz) % 4) * 8 + ((py + oy) % 4) * 2 + (pc + oc) % 2

    barrier = pltpu.get_barrier_semaphore()

    def greet(i, carry):
        pl.semaphore_signal(barrier, inc=1, device_id=peer(i), device_id_type=MESH)
        return carry

    lax.fori_loop(0, DEV - 1, greet, 0)

    sub = lax.broadcasted_iota(jnp.int32, (128, 128), 0)
    lane = lax.broadcasted_iota(jnp.int32, (128, 128), 1)
    sub8 = lax.broadcasted_iota(jnp.int32, (8, 128), 0)

    def send(index):
        def one(i, carry):
            tx, ty = peer(i)
            pltpu.make_async_remote_copy(
                src_ref=snd.at[index, tx * 32 + ty], dst_ref=rcv.at[index, me],
                send_sem=snd_sem.at[index], recv_sem=rcv_sem.at[index],
                device_id=(tx, ty), device_id_type=MESH,
            ).start()
            return carry

        lax.fori_loop(0, DEV - 1, one, 0)
        rcv[index, pl.ds(me, 1), :] = snd[index, pl.ds(me, 1), :]

    def receive(index):
        rows = pl.ds(0, DEV - 1)
        pltpu.make_async_copy(
            snd.at[index, rows], rcv.at[index, rows], rcv_sem.at[index]
        ).wait()
        return rcv[index].T

    def sent(index):
        rows = pl.ds(0, DEV - 1)
        pltpu.make_async_copy(
            snd.at[index, rows], rcv.at[index, rows], snd_sem.at[index]
        ).wait()

    def post(index, dots=()):
        for j, value in enumerate(dots):
            mt[16 + j : 17 + j, :] = jnp.broadcast_to(value, (1, 128))
        snd[index] = mt[...].T
        send(index)

    def lane_sum(received, j):
        return jnp.sum(received[16 + j : 17 + j], axis=1, keepdims=True)

    mt[...] = jnp.zeros((128, 128), F32)
    pads[...] = jnp.zeros((2, 128, 128), jnp.int32)
    pads[0, :, 0:CAP] = cell_ref[0]
    pads[1, :, 0:CAP] = slot_ref[0]
    cells = pads[0].astype(F32).T[0:16].astype(jnp.int32)
    slots = pads[1].astype(F32).T[0:16].astype(jnp.int32)
    row_of = lax.shift_right_logical(cells, 7)
    col_of = lax.bitwise_and(cells, 127)
    well_of = lax.shift_right_logical(slots, 7)
    seg_of = lax.bitwise_and(slots, 127)
    for q in range(CAP):
        part = slice(q * 128, (q + 1) * 128)
        hot = jnp.where(sub == row_of[q : q + 1], 1.0, 0.0).astype(BF16)
        oht[0:128, part] = hot
        oht[128:256, part] = hot
        cmt[:, part] = jnp.where(sub == col_of[q : q + 1], 1.0, 0.0)
        seg_hot = jnp.where(sub == seg_of[q : q + 1], 1.0, 0.0)
        gt[:, part] = seg_hot.astype(BF16)
        gts[part, :] = seg_hot.T.astype(BF16)
        wmask[:, part] = jnp.where(sub8 == well_of[q : q + 1], 1.0, 0.0)
    vals[...] = jnp.zeros((48, 128), F32)
    for w in range(8):
        high, low = split(winv_ref[w].T)
        part = slice(w * 128, (w + 1) * 128)
        w2[0:128, part] = high.astype(BF16)
        w2[128:256, part] = low.astype(BF16)

    inner = lax.bitwise_and(sub, 15)
    layer = lax.shift_right_logical(sub, 4)
    outside = (
        (inner == 0) & (gx == 0),
        (inner == 15) & (gx == 3),
        (lane == 0) & (gy == 0),
        (lane == 127) & (gy == 31),
        layer == 0,
        layer == 7,
    )
    for n in range(6):
        faces[n] = jnp.where(outside[n], 0.0, flat(face_ref[n].astype(F32)))

    def gather(fields):
        stacked = jnp.concatenate([field.T for field in fields], axis=0)
        high, low = split(stacked)
        pair = jnp.concatenate([high.astype(BF16), low.astype(BF16)], axis=1)
        for q in range(0, CAP, 2):
            part = slice(q * 128, (q + 2) * 128)
            picked = dot(pair, oht[:, part])
            mask = cmt[:, part]
            for c in range(3):
                value = jnp.sum(picked[c * 128 : (c + 1) * 128] * mask, axis=0, keepdims=True)
                vals[c * 16 + q : c * 16 + q + 1, :] = value[:, 0:128]
                vals[c * 16 + q + 1 : c * 16 + q + 2, :] = value[:, 128:256]

    def by_slot(rows):
        high, low = split(rows)
        both = jnp.concatenate([high, low], axis=0).astype(BF16)
        spread = dot(both, gt[...])
        count = rows.shape[0]
        spread = spread[0:count] + spread[count:]
        return [
            jnp.sum(spread[n : n + 8] * wmask[...], axis=0, keepdims=True)
            for n in range(0, count, 8)
        ]

    def put_rows(ref, base, row):
        for q in range(CAP):
            ref[base + q : base + q + 1, :] = row[:, q * 128 : (q + 1) * 128]

    def solve_wells(rate):
        spread = jnp.concatenate(
            [jnp.broadcast_to(rate[q : q + 1], (8, 128)) for q in range(CAP)], axis=1
        ) * wmask[...]
        high, low = split(spread)
        totals = dot(jnp.concatenate([high, low], axis=0).astype(BF16), gts[...])
        high, low = split(totals[0:8] + totals[8:16])
        left = jnp.concatenate(
            [
                jnp.concatenate([high, high], axis=1),
                jnp.concatenate([low, jnp.zeros_like(low)], axis=1),
            ],
            axis=0,
        ).astype(BF16)
        product = dot(left, w2[...])
        product = product[0:8] + product[8:16]
        seg = jnp.zeros((8, 128), F32)
        for w in range(8):
            seg = jnp.where(sub8 == w, product[:, w * 128 : (w + 1) * 128], seg)
        put_rows(mt, 0, by_slot(seg)[0])

    def scatter(back):
        pieces = []
        for c in range(3):
            pieces.append(split(coef[3 + c] * back))
        stacked = []
        for half in range(2):
            for q in range(CAP):
                mask = cmt[:, q * 128 : (q + 1) * 128]
                stacked.append(
                    jnp.concatenate(
                        [mask * pieces[c][half][q : q + 1] for c in range(3)], axis=0
                    ).astype(BF16)
                )
        right = jnp.concatenate(stacked, axis=1)
        left = jnp.concatenate([oht[0:128], oht[0:128]], axis=1)
        term = dot_nt(left, right)
        return [term[:, c * 128 : (c + 1) * 128] for c in range(3)]

    def couple(ref, fields, a):
        out = flat(ref[:, a, 0].astype(F32)) * fields[0]
        out = out + flat(ref[:, a, 1].astype(F32)) * fields[1]
        return out + flat(ref[:, a, 2].astype(F32)) * fields[2]

    def halo_copies(op):
        low, high = (gx + 3) % 4, (gx + 1) % 4
        left, right = (gy + 31) % 32, (gy + 1) % 32

        def row_copy(mine, theirs, which, target):
            return pltpu.make_async_remote_copy(
                src_ref=flux_pad.at[op, :, :, mine], dst_ref=flux_pad.at[op, :, :, theirs],
                send_sem=hs_sem.at[op, which], recv_sem=hr_sem.at[op, which],
                device_id=(target, gy), device_id_type=MESH,
            )

        def col_copy(which, target):
            return pltpu.make_async_remote_copy(
                src_ref=col_snd.at[op], dst_ref=col_rcv.at[op, which],
                send_sem=hs_sem.at[op, 2 + which], recv_sem=hr_sem.at[op, 2 + which],
                device_id=(gx, target), device_id_type=MESH,
            )

        return (
            row_copy(23, 7, 0, high),
            row_copy(8, 24, 1, low),
            col_copy(0, right),
            col_copy(1, left),
        )

    def stencil_start(op, fields):
        fluxes = [couple(mob_ref, fields, a) for a in range(3)]
        packed = jnp.zeros((128, 128), F32)
        for a in range(3):
            flux_pad[op, a, :, 8:24, :] = fluxes[a].reshape(8, 16, 128)
            packed = jnp.where(lane == a, fluxes[a][:, 127:128], packed)
            packed = jnp.where(lane == 3 + a, fluxes[a][:, 0:1], packed)
        col_snd[op] = packed.T[0:8]
        copies = halo_copies(op)
        for copy in copies:
            copy.start()
        centre = []
        for a in range(3):
            flux = fluxes[a]
            zero = jnp.zeros((16, 128), F32)
            out = couple(diag_ref, fields, a)
            out = out - faces[4] * jnp.concatenate([zero, flux[0:112]], axis=0)
            out = out - faces[5] * jnp.concatenate([flux[16:128], zero], axis=0)
            centre.append(out)
        return copies, centre

    def stencil_end(op, copies, centre):
        for copy in copies:
            copy.wait()
        edge_low = jnp.concatenate([col_rcv[op, 0], jnp.zeros((120, 128), F32)], axis=0).T
        edge_high = jnp.concatenate([col_rcv[op, 1], jnp.zeros((120, 128), F32)], axis=0).T
        outs = []
        for a in range(3):
            flux = flat(flux_pad[op, a, :, 8:24, :])
            before = jnp.where(lane == 0, edge_low[:, a : a + 1], pltpu.roll(flux, 1, 1))
            after = jnp.where(lane == 127, edge_high[:, 3 + a : 4 + a], pltpu.roll(flux, 127, 1))
            out = centre[a] - faces[0] * flat(flux_pad[op, a, :, 7:23, :])
            out = out - faces[1] * flat(flux_pad[op, a, :, 9:25, :])
            out = out - faces[2] * before
            outs.append(out - faces[3] * after)
        return outs

    def precondition(fields):
        paired = [field.reshape(4, 2, 16, 128) for field in fields]
        results = []
        for e in range(6):
            total = None
            for f in range(6):
                term = colinv_ref[:, e, f].astype(F32) * paired[f % 3][:, f // 3]
                total = term if total is None else total + term
            results.append(total)
        return [
            flat(jnp.concatenate([results[c][:, None], results[3 + c][:, None]], axis=1))
            for c in range(3)
        ]

    def combine(scale, xs, ys):
        return [x + scale * y for x, y in zip(xs, ys)]

    guess = [flat(guess_ref[:, c]) for c in range(3)]
    gather(guess)
    mt[0:48, :] = vals[...]
    snd[0] = mt[...].T
    pl.semaphore_wait(barrier, DEV - 1)
    send(0)
    started = stencil_start(0, guess)
    rows = [win_ref[c : c + 1, w * 128 : (w + 1) * 128] for c in range(3) for w in range(8)]
    rows += [wout_ref[c : c + 1, w * 128 : (w + 1) * 128] for c in range(3) for w in range(8)]
    own = by_slot(jnp.concatenate(rows, axis=0))
    mt[...] = jnp.zeros((128, 128), F32)
    for n in range(6):
        put_rows(mt, 16 + n * 16, own[n])
    got = receive(0)
    rate = sum(mt[16 + 16 * c : 32 + 16 * c, :] * got[16 * c : 16 * c + 16] for c in range(3))
    solve_wells(rate)
    post(1)
    applied = stencil_end(0, *started)
    got = receive(1)
    for n in range(6):
        coef[n] = got[16 + 16 * n : 32 + 16 * n]
    term = scatter(got[0:16])
    r0 = [flat(right_ref[:, c]) - (applied[c] - term[c]) for c in range(3)]

    def operate(op, fields, dots, on_first=None):
        gather(fields)
        mt[0:16, :] = coef[0] * vals[0:16] + coef[1] * vals[16:32] + coef[2] * vals[32:48]
        post(2 * op, dots)
        started = stencil_start(op, fields)
        got = receive(2 * op)
        sums = [lane_sum(got, j) for j in range(len(dots))]
        solve_wells(got[0:16])
        extra = () if on_first is None else on_first(sums)
        post(2 * op + 1, extra)
        applied = stencil_end(op, *started)
        got = receive(2 * op + 1)
        late = [lane_sum(got, j) for j in range(len(extra))]
        term = scatter(got[0:16])
        return [applied[c] - term[c] for c in range(3)], sums, late

    u1 = precondition(r0)
    v0, (rho0,), _ = operate(1, u1, [local_sum(r0, r0)])
    u2 = precondition(v0)
    y0, (projected,), _ = operate(2, u2, [local_sum(r0, v0)])
    alpha0 = rho0 / projected
    s0 = combine(-alpha0, r0, v0)
    t0 = combine(-alpha0, v0, y0)
    u3 = precondition(t0)

    def new_rho(sums):
        r1 = combine(-(sums[0] / sums[1]), s0, t0)
        return [local_sum(r0, r1)]

    w0, (cross0, self0), (rho1,) = operate(
        3, u3, [local_sum(t0, s0), local_sum(t0, t0)], new_rho
    )
    omega0 = cross0 / self0
    beta = rho1 / rho0 * (alpha0 / omega0)
    r1 = combine(-omega0, s0, t0)
    a_r1 = combine(-omega0, t0, w0)
    v1 = combine(beta, a_r1, combine(-omega0, v0, y0))
    u4 = precondition(v1)
    y1, (projected1,), _ = operate(4, u4, [local_sum(r0, v1)])
    alpha1 = rho1 / projected1
    s1 = combine(-alpha1, r1, v1)
    t1 = combine(-alpha1, a_r1, y1)
    post(10, [local_sum(t1, s1), local_sum(t1, t1)])
    ms0 = combine(-alpha0, u1, u2)
    mr1 = combine(-omega0, ms0, u3)
    mp1 = combine(beta, mr1, combine(-omega0, u1, u2))
    ms1 = combine(-alpha1, mr1, u4)
    guess = [flat(guess_ref[:, c]) for c in range(3)]
    partial = combine(alpha1, combine(omega0, combine(alpha0, guess, u1), ms0), mp1)
    got = receive(10)
    omega1 = lane_sum(got, 0) / lane_sum(got, 1)
    final = combine(omega1, partial, ms1)
    left = combine(-omega1, s1, t1)
    for c in range(3):
        sol_ref[:, c] = final[c].reshape(8, 16, 128)
        res_ref[:, c] = left[c].reshape(8, 16, 128)
    for index in range(EXCHANGES):
        sent(index)


def per_device(*args):
    shape = args[0].shape
    vmem = pl.BlockSpec(memory_space=pltpu.VMEM)
    return pl.pallas_call(
        kernel,
        out_shape=(jax.ShapeDtypeStruct(shape, F32), jax.ShapeDtypeStruct(shape, F32)),
        in_specs=[vmem] * 11,
        out_specs=(vmem, vmem),
        scratch_shapes=[
            pltpu.VMEM((EXCHANGES, 128, 128), F32),
            pltpu.VMEM((EXCHANGES, 128, 128), F32),
            pltpu.VMEM((OPS, 3, 8, 32, 128), F32),
            pltpu.VMEM((OPS, 8, 128), F32),
            pltpu.VMEM((OPS, 2, 8, 128), F32),
            pltpu.VMEM((128, 128), F32),
            pltpu.VMEM((2, 128, 128), jnp.int32),
            pltpu.VMEM((6, 128, 128), F32),
            pltpu.VMEM((256, SLOTS), BF16),
            pltpu.VMEM((128, SLOTS), F32),
            pltpu.VMEM((SLOTS, 128), BF16),
            pltpu.VMEM((128, SLOTS), BF16),
            pltpu.VMEM((8, SLOTS), F32),
            pltpu.VMEM((256, 1024), BF16),
            pltpu.VMEM((48, 128), F32),
            pltpu.VMEM((6, 16, 128), F32),
            pltpu.SemaphoreType.DMA((EXCHANGES,)),
            pltpu.SemaphoreType.DMA((EXCHANGES,)),
            pltpu.SemaphoreType.DMA((OPS, 4)),
            pltpu.SemaphoreType.DMA((OPS, 4)),
        ],
        compiler_params=pltpu.CompilerParams(
            collective_id=0, has_side_effects=True, vmem_limit_bytes=48 * 1024 * 1024
        ),
    )(*args)


def solution(mesh):
    in_specs = (
        P(None, None, "gx", "gy"),
        P(None, None, "gx", "gy"),
        P(None, None, None, "gx", "gy"),
        P(None, None, None, "gx", "gy"),
        P(None, None, "gx", "gy"),
        P(None, None, None, "gx", "gy"),
        P(("gx", "gy"), None, None),
        P(("gx", "gy"), None, None),
        P(None, ("gx", "gy")),
        P(None, ("gx", "gy")),
        P(("gx", "gy"), None, None),
    )
    out_specs = (P(None, None, "gx", "gy"), P(None, None, "gx", "gy"))
    return jax.shard_map(
        per_device, mesh=mesh, in_specs=in_specs, out_specs=out_specs, check_vma=False
    )
```

```python
import jax
import jax.numpy as jnp
from jax import lax
from jax.experimental import pallas as pl
from jax.experimental.pallas import tpu as pltpu
from jax.sharding import PartitionSpec as P

MESH = pl.DeviceIdType.MESH
F32 = jnp.float32
BF16 = jnp.bfloat16
DEV = 128
CAP = 10
FAR_FIRST = (2, 3, 1, 0)
SLOTS = DEV * CAP
OPS = 5
EXCHANGES = 2 * OPS + 1


def dot(a, b):
    return lax.dot_general(a, b, (((1,), (0,)), ((), ())), preferred_element_type=F32)


def dot_nt(a, b):
    return lax.dot_general(a, b, (((1,), (1,)), ((), ())), preferred_element_type=F32)


def split(value):
    high = value.astype(BF16).astype(F32)
    return high, value - high


def flat(value):
    return value.reshape(128, 128)


def local_sum(lefts, rights):
    total = lefts[0] * rights[0] + lefts[1] * rights[1] + lefts[2] * rights[2]
    return jnp.sum(jnp.sum(total, axis=0, keepdims=True), axis=1, keepdims=True)


def kernel(
    right_in, guess_in, diag_in, mob_in, face_in, colinv_in, cell_in, slot_in, win_in, wout_in,
    winv_in, sol_ref, res_ref,
    right_ref, guess_ref, diag_ref, mob_ref, face_ref, colinv_ref, cell_ref, slot_ref, win_ref,
    wout_ref, winv_ref, load_sem,
    snd, rcv, flux_pad, col_snd, col_rcv, mt, faces, oht, cmt, gts, gt, wmask, w2, vals, coef,
    snd_sem, rcv_sem, hs_sem, hr_sem,
):
    gx = lax.axis_index("gx")
    gy = lax.axis_index("gy")
    me = gx * 32 + gy
    pz, py, pc = lax.div(gy, 8), lax.rem(lax.div(gy, 2), 4), lax.rem(gy, 2)
    near = [
        (oy, oc, lax.rem(py + oy, 4) * 2 + (1 - pc if oc else pc)) for oy in FAR_FIRST for oc in (1, 0)
    ]

    def every_peer(act):
        def some(i, carry):
            tx, tz = 3 - lax.div(i, 4), 3 - lax.rem(i, 4)
            dx = lax.rem(gx + lax.div(tx * (tx + 1), 2), 4)
            dz = lax.rem(pz + lax.div(tz * (tz + 1), 2), 4) * 8
            for _, _, low in near:
                act(dx, dz + low)
            return carry

        lax.fori_loop(0, 15, some, 0)
        for oy, oc, low in near:
            if oy or oc:
                act(gx, pz * 8 + low)

    barrier = pltpu.get_barrier_semaphore()

    def greet(tx, ty):
        pl.semaphore_signal(barrier, inc=1, device_id=(tx, ty), device_id_type=MESH)

    every_peer(greet)
    loads = {}
    for n, (name, src, dst) in enumerate((
        ("cell", cell_in, cell_ref), ("guess", guess_in, guess_ref), ("slot", slot_in, slot_ref),
        ("winv", winv_in, winv_ref), ("face", face_in, face_ref), ("win", win_in, win_ref),
        ("wout", wout_in, wout_ref), ("mob", mob_in, mob_ref), ("diag", diag_in, diag_ref),
        ("right", right_in, right_ref), ("colinv", colinv_in, colinv_ref),
    )):
        loads[name] = pltpu.make_async_copy(src, dst, load_sem.at[n])
        loads[name].start()

    sub = lax.broadcasted_iota(jnp.int32, (128, 128), 0)
    lane = lax.broadcasted_iota(jnp.int32, (128, 128), 1)
    sub8 = lax.broadcasted_iota(jnp.int32, (8, 128), 0)

    def send(index):
        def one(tx, ty):
            pltpu.make_async_remote_copy(
                src_ref=snd.at[index, tx * 32 + ty], dst_ref=rcv.at[index, me],
                send_sem=snd_sem.at[index], recv_sem=rcv_sem.at[index],
                device_id=(tx, ty), device_id_type=MESH,
            ).start()

        every_peer(one)
        rcv[index, pl.ds(me, 1), :] = snd[index, pl.ds(me, 1), :]

    def receive(index):
        rows = pl.ds(0, DEV - 1)
        pltpu.make_async_copy(
            snd.at[index, rows], rcv.at[index, rows], rcv_sem.at[index]
        ).wait()
        return rcv[index].T

    def sent(index):
        rows = pl.ds(0, DEV - 1)
        pltpu.make_async_copy(
            snd.at[index, rows], rcv.at[index, rows], snd_sem.at[index]
        ).wait()

    def post(index, dots=()):
        for j, value in enumerate(dots):
            mt[16 + j : 17 + j, :] = jnp.broadcast_to(value, (1, 128))
        snd[index] = mt[...].T
        send(index)

    def lane_sum(received, j):
        return jnp.sum(received[16 + j : 17 + j], axis=1, keepdims=True)

    mt[...] = jnp.zeros((128, 128), F32)
    loads["cell"].wait()
    cells = cell_ref[:, 0, :]
    row_of = lax.shift_right_logical(cells, 7)
    col_of = lax.bitwise_and(cells, 127)
    for q in range(CAP):
        part = slice(q * 128, (q + 1) * 128)
        hot = jnp.where(sub == row_of[q : q + 1], 1.0, 0.0).astype(BF16)
        oht[0:128, part] = hot
        oht[128:256, part] = hot
        cmt[:, part] = jnp.where(sub == col_of[q : q + 1], 1.0, 0.0)
    vals[...] = jnp.zeros((48, 128), F32)
    loads["slot"].wait()
    slots = slot_ref[:, 0, :]
    well_of = lax.shift_right_logical(slots, 7)
    seg_of = lax.bitwise_and(slots, 127)
    for q in range(CAP):
        part = slice(q * 128, (q + 1) * 128)
        seg_hot = jnp.where(sub == seg_of[q : q + 1], 1.0, 0.0)
        gt[:, part] = seg_hot.astype(BF16)
        gts[part, :] = seg_hot.T.astype(BF16)
        wmask[:, part] = jnp.where(sub8 == well_of[q : q + 1], 1.0, 0.0)
    loads["winv"].wait()
    for w in range(8):
        high, low = split(winv_ref[w].T)
        part = slice(w * 128, (w + 1) * 128)
        w2[0:128, part] = high.astype(BF16)
        w2[128:256, part] = low.astype(BF16)

    inner = lax.bitwise_and(sub, 15)
    layer = lax.shift_right_logical(sub, 4)
    outside = (
        (inner == 0) & (gx == 0),
        (inner == 15) & (gx == 3),
        (lane == 0) & (gy == 0),
        (lane == 127) & (gy == 31),
        layer == 0,
        layer == 7,
    )
    loads["face"].wait()
    for n in range(6):
        faces[n] = jnp.where(outside[n], 0.0, flat(face_ref[n].astype(F32)))

    def gather(fields):
        stacked = jnp.concatenate([field.T for field in fields], axis=0)
        high, low = split(stacked)
        pair = jnp.concatenate([high.astype(BF16), low.astype(BF16)], axis=1)
        for q in range(0, CAP, 2):
            part = slice(q * 128, (q + 2) * 128)
            picked = dot(pair, oht[:, part])
            mask = cmt[:, part]
            for c in range(3):
                value = jnp.sum(picked[c * 128 : (c + 1) * 128] * mask, axis=0, keepdims=True)
                vals[c * 16 + q : c * 16 + q + 1, :] = value[:, 0:128]
                vals[c * 16 + q + 1 : c * 16 + q + 2, :] = value[:, 128:256]

    def by_slot(rows):
        high, low = split(rows)
        both = jnp.concatenate([high, low], axis=0).astype(BF16)
        spread = dot(both, gt[...])
        count = rows.shape[0]
        spread = spread[0:count] + spread[count:]
        return [
            jnp.sum(spread[n : n + 8] * wmask[...], axis=0, keepdims=True)
            for n in range(0, count, 8)
        ]

    def put_rows(ref, base, row):
        for q in range(CAP):
            ref[base + q : base + q + 1, :] = row[:, q * 128 : (q + 1) * 128]

    def solve_wells(rate):
        spread = jnp.concatenate(
            [jnp.broadcast_to(rate[q : q + 1], (8, 128)) for q in range(CAP)], axis=1
        ) * wmask[...]
        high, low = split(spread)
        totals = dot(jnp.concatenate([high, low], axis=0).astype(BF16), gts[...])
        high, low = split(totals[0:8] + totals[8:16])
        left = jnp.concatenate(
            [
                jnp.concatenate([high, high], axis=1),
                jnp.concatenate([low, jnp.zeros_like(low)], axis=1),
            ],
            axis=0,
        ).astype(BF16)
        product = dot(left, w2[...])
        product = product[0:8] + product[8:16]
        seg = jnp.zeros((8, 128), F32)
        for w in range(8):
            seg = jnp.where(sub8 == w, product[:, w * 128 : (w + 1) * 128], seg)
        put_rows(mt, 0, by_slot(seg)[0])

    def scatter(back):
        pieces = []
        for c in range(3):
            pieces.append(split(coef[3 + c] * back))
        stacked = []
        for half in range(2):
            for q in range(CAP):
                mask = cmt[:, q * 128 : (q + 1) * 128]
                stacked.append(
                    jnp.concatenate(
                        [mask * pieces[c][half][q : q + 1] for c in range(3)], axis=0
                    ).astype(BF16)
                )
        right = jnp.concatenate(stacked, axis=1)
        left = jnp.concatenate([oht[0:128], oht[0:128]], axis=1)
        term = dot_nt(left, right)
        return [term[:, c * 128 : (c + 1) * 128] for c in range(3)]

    def couple(ref, fields, a):
        out = flat(ref[:, a, 0].astype(F32)) * fields[0]
        out = out + flat(ref[:, a, 1].astype(F32)) * fields[1]
        return out + flat(ref[:, a, 2].astype(F32)) * fields[2]

    def halo_copies(op):
        low, high = (gx + 3) % 4, (gx + 1) % 4
        left, right = (gy + 31) % 32, (gy + 1) % 32

        def row_copy(mine, theirs, which, target):
            return pltpu.make_async_remote_copy(
                src_ref=flux_pad.at[op, :, :, mine], dst_ref=flux_pad.at[op, :, :, theirs],
                send_sem=hs_sem.at[op, which], recv_sem=hr_sem.at[op, which],
                device_id=(target, gy), device_id_type=MESH,
            )

        def col_copy(which, target):
            return pltpu.make_async_remote_copy(
                src_ref=col_snd.at[op], dst_ref=col_rcv.at[op, which],
                send_sem=hs_sem.at[op, 2 + which], recv_sem=hr_sem.at[op, 2 + which],
                device_id=(gx, target), device_id_type=MESH,
            )

        return (
            row_copy(23, 7, 0, high),
            row_copy(8, 24, 1, low),
            col_copy(0, right),
            col_copy(1, left),
        )

    def stencil_start(op, fields):
        fluxes = [couple(mob_ref, fields, a) for a in range(3)]
        packed = jnp.zeros((128, 128), F32)
        for a in range(3):
            flux_pad[op, a, :, 8:24, :] = fluxes[a].reshape(8, 16, 128)
            packed = jnp.where(lane == a, fluxes[a][:, 127:128], packed)
            packed = jnp.where(lane == 3 + a, fluxes[a][:, 0:1], packed)
        col_snd[op] = packed.T[0:8]
        copies = halo_copies(op)
        for copy in copies:
            copy.start()
        centre = []
        for a in range(3):
            flux = fluxes[a]
            zero = jnp.zeros((16, 128), F32)
            out = couple(diag_ref, fields, a)
            out = out - faces[4] * jnp.concatenate([zero, flux[0:112]], axis=0)
            out = out - faces[5] * jnp.concatenate([flux[16:128], zero], axis=0)
            centre.append(out)
        return copies, centre

    def stencil_end(op, copies, centre):
        for copy in copies:
            copy.wait()
        edge_low = jnp.concatenate([col_rcv[op, 0], jnp.zeros((120, 128), F32)], axis=0).T
        edge_high = jnp.concatenate([col_rcv[op, 1], jnp.zeros((120, 128), F32)], axis=0).T
        outs = []
        for a in range(3):
            flux = flat(flux_pad[op, a, :, 8:24, :])
            before = jnp.where(lane == 0, edge_low[:, a : a + 1], pltpu.roll(flux, 1, 1))
            after = jnp.where(lane == 127, edge_high[:, 3 + a : 4 + a], pltpu.roll(flux, 127, 1))
            out = centre[a] - faces[0] * flat(flux_pad[op, a, :, 7:23, :])
            out = out - faces[1] * flat(flux_pad[op, a, :, 9:25, :])
            out = out - faces[2] * before
            outs.append(out - faces[3] * after)
        return outs

    def precondition(fields):
        paired = [field.reshape(4, 2, 16, 128) for field in fields]
        results = []
        for e in range(6):
            total = None
            for f in range(6):
                term = colinv_ref[:, e, f].astype(F32) * paired[f % 3][:, f // 3]
                total = term if total is None else total + term
            results.append(total)
        return [
            flat(jnp.concatenate([results[c][:, None], results[3 + c][:, None]], axis=1))
            for c in range(3)
        ]

    def combine(scale, xs, ys):
        return [x + scale * y for x, y in zip(xs, ys)]

    loads["guess"].wait()
    guess = [flat(guess_ref[:, c]) for c in range(3)]
    gather(guess)
    mt[0:48, :] = vals[...]
    snd[0] = mt[...].T
    for name in ("win", "wout", "mob", "diag", "right", "colinv"):
        loads[name].wait()
    pl.semaphore_wait(barrier, DEV - 1)
    send(0)
    started = stencil_start(0, guess)
    rows = [win_ref[c : c + 1, w * 128 : (w + 1) * 128] for c in range(3) for w in range(8)]
    rows += [wout_ref[c : c + 1, w * 128 : (w + 1) * 128] for c in range(3) for w in range(8)]
    own = by_slot(jnp.concatenate(rows, axis=0))
    mt[...] = jnp.zeros((128, 128), F32)
    for n in range(6):
        put_rows(mt, 16 + n * 16, own[n])
    got = receive(0)
    rate = sum(mt[16 + 16 * c : 32 + 16 * c, :] * got[16 * c : 16 * c + 16] for c in range(3))
    solve_wells(rate)
    post(1)
    applied = stencil_end(0, *started)
    got = receive(1)
    for n in range(6):
        coef[n] = got[16 + 16 * n : 32 + 16 * n]
    term = scatter(got[0:16])
    r0 = [flat(right_ref[:, c]) - (applied[c] - term[c]) for c in range(3)]

    def operate(op, fields, dots, on_first=None):
        gather(fields)
        mt[0:16, :] = coef[0] * vals[0:16] + coef[1] * vals[16:32] + coef[2] * vals[32:48]
        post(2 * op, dots)
        started = stencil_start(op, fields)
        got = receive(2 * op)
        sums = [lane_sum(got, j) for j in range(len(dots))]
        solve_wells(got[0:16])
        extra = () if on_first is None else on_first(sums)
        post(2 * op + 1, extra)
        applied = stencil_end(op, *started)
        got = receive(2 * op + 1)
        late = [lane_sum(got, j) for j in range(len(extra))]
        term = scatter(got[0:16])
        return [applied[c] - term[c] for c in range(3)], sums, late

    u1 = precondition(r0)
    v0, (rho0,), _ = operate(1, u1, [local_sum(r0, r0)])
    u2 = precondition(v0)
    y0, (projected,), _ = operate(2, u2, [local_sum(r0, v0)])
    alpha0 = rho0 / projected
    s0 = combine(-alpha0, r0, v0)
    t0 = combine(-alpha0, v0, y0)
    u3 = precondition(t0)

    def new_rho(sums):
        r1 = combine(-(sums[0] / sums[1]), s0, t0)
        return [local_sum(r0, r1)]

    w0, (cross0, self0), (rho1,) = operate(
        3, u3, [local_sum(t0, s0), local_sum(t0, t0)], new_rho
    )
    omega0 = cross0 / self0
    beta = rho1 / rho0 * (alpha0 / omega0)
    r1 = combine(-omega0, s0, t0)
    a_r1 = combine(-omega0, t0, w0)
    v1 = combine(beta, a_r1, combine(-omega0, v0, y0))
    u4 = precondition(v1)
    y1, (projected1,), _ = operate(4, u4, [local_sum(r0, v1)])
    alpha1 = rho1 / projected1
    s1 = combine(-alpha1, r1, v1)
    t1 = combine(-alpha1, a_r1, y1)
    post(10, [local_sum(t1, s1), local_sum(t1, t1)])
    ms0 = combine(-alpha0, u1, u2)
    mr1 = combine(-omega0, ms0, u3)
    mp1 = combine(beta, mr1, combine(-omega0, u1, u2))
    ms1 = combine(-alpha1, mr1, u4)
    guess = [flat(guess_ref[:, c]) for c in range(3)]
    partial = combine(alpha1, combine(omega0, combine(alpha0, guess, u1), ms0), mp1)
    got = receive(10)
    omega1 = lane_sum(got, 0) / lane_sum(got, 1)
    final = combine(omega1, partial, ms1)
    left = combine(-omega1, s1, t1)
    for c in range(3):
        sol_ref[:, c] = final[c].reshape(8, 16, 128)
        res_ref[:, c] = left[c].reshape(8, 16, 128)
    for index in range(EXCHANGES):
        sent(index)


def per_device(*args):
    args = list(args)
    for n in (6, 7):
        args[n] = jnp.transpose(args[n], (2, 0, 1))
    shape = args[0].shape
    hbm = pl.BlockSpec(memory_space=pltpu.HBM)
    vmem = pl.BlockSpec(memory_space=pltpu.VMEM)
    return pl.pallas_call(
        kernel,
        out_shape=(jax.ShapeDtypeStruct(shape, F32), jax.ShapeDtypeStruct(shape, F32)),
        in_specs=[hbm] * 11,
        out_specs=(vmem, vmem),
        scratch_shapes=[pltpu.VMEM(arg.shape, arg.dtype) for arg in args]
        + [
            pltpu.SemaphoreType.DMA((11,)),
            pltpu.VMEM((EXCHANGES, 128, 128), F32),
            pltpu.VMEM((EXCHANGES, 128, 128), F32),
            pltpu.VMEM((OPS, 3, 8, 32, 128), F32),
            pltpu.VMEM((OPS, 8, 128), F32),
            pltpu.VMEM((OPS, 2, 8, 128), F32),
            pltpu.VMEM((128, 128), F32),
            pltpu.VMEM((6, 128, 128), F32),
            pltpu.VMEM((256, SLOTS), BF16),
            pltpu.VMEM((128, SLOTS), F32),
            pltpu.VMEM((SLOTS, 128), BF16),
            pltpu.VMEM((128, SLOTS), BF16),
            pltpu.VMEM((8, SLOTS), F32),
            pltpu.VMEM((256, 1024), BF16),
            pltpu.VMEM((48, 128), F32),
            pltpu.VMEM((6, 16, 128), F32),
            pltpu.SemaphoreType.DMA((EXCHANGES,)),
            pltpu.SemaphoreType.DMA((EXCHANGES,)),
            pltpu.SemaphoreType.DMA((OPS, 4)),
            pltpu.SemaphoreType.DMA((OPS, 4)),
        ],
        compiler_params=pltpu.CompilerParams(
            collective_id=0, has_side_effects=True, vmem_limit_bytes=60 * 1024 * 1024
        ),
    )(*args)


def solution(mesh):
    in_specs = (
        P(None, None, "gx", "gy"),
        P(None, None, "gx", "gy"),
        P(None, None, None, "gx", "gy"),
        P(None, None, None, "gx", "gy"),
        P(None, None, "gx", "gy"),
        P(None, None, None, "gx", "gy"),
        P(("gx", "gy"), None, None),
        P(("gx", "gy"), None, None),
        P(None, ("gx", "gy")),
        P(None, ("gx", "gy")),
        P(("gx", "gy"), None, None),
    )
    out_specs = (P(None, None, "gx", "gy"), P(None, None, "gx", "gy"))
    return jax.shard_map(
        per_device, mesh=mesh, in_specs=in_specs, out_specs=out_specs, check_vma=False
    )
```

```python
import jax
import jax.numpy as jnp
from jax import lax
from jax.experimental import pallas as pl
from jax.experimental.pallas import tpu as pltpu
from jax.sharding import PartitionSpec as P

MESH = pl.DeviceIdType.MESH
F32 = jnp.float32
BF16 = jnp.bfloat16
DEV = 128
CAP = 10
FAR_FIRST = (2, 3, 1, 0)
SLOTS = DEV * CAP
OPS = 5
EXCHANGES = 2 * OPS + 1


def dot(a, b):
    return lax.dot_general(a, b, (((1,), (0,)), ((), ())), preferred_element_type=F32)


def dot_nt(a, b):
    return lax.dot_general(a, b, (((1,), (1,)), ((), ())), preferred_element_type=F32)


def split(value):
    high = value.astype(BF16).astype(F32)
    return high, value - high


def flat(value):
    return value.reshape(128, 128)


def local_sum(lefts, rights):
    total = lefts[0] * rights[0] + lefts[1] * rights[1] + lefts[2] * rights[2]
    return jnp.sum(jnp.sum(total, axis=0, keepdims=True), axis=1, keepdims=True)


def kernel(
    right_in, guess_in, diag_in, mob_in, face_in, colinv_in, cell_in, slot_in, win_in, wout_in,
    winv_in, sol_ref, res_ref,
    right_ref, guess_ref, diag_ref, mob_ref, face_ref, colinv_ref, cell_ref, slot_ref, win_ref,
    wout_ref, winv_ref, load_sem,
    snd, rcv, flux_pad, col_snd, col_rcv, mt, faces, oht, cmt, cmb, terms, gts, gt, wmask, solver, vals, coef, link,
    link_w, link_a, link_out,
    snd_sem, rcv_sem, hs_sem, hr_sem,
):
    gx = lax.axis_index("gx")
    gy = lax.axis_index("gy")
    me = gx * 32 + gy
    pz, py, pc = lax.div(gy, 8), lax.rem(lax.div(gy, 2), 4), lax.rem(gy, 2)
    near = [
        (oy, oc, lax.rem(py + oy, 4) * 2 + (1 - pc if oc else pc)) for oy in FAR_FIRST for oc in (1, 0)
    ]

    xs = [lax.rem(gx + o, 4) for o in range(4)]
    zs = [lax.rem(pz + o, 4) * 8 for o in range(4)]

    def every_peer(act):
        for ox in FAR_FIRST:
            for oz in FAR_FIRST:
                for oy, oc, low in near:
                    if ox or oz or oy or oc:
                        act(xs[ox], zs[oz] + low)

    barrier = pltpu.get_barrier_semaphore()

    def greet(tx, ty):
        pl.semaphore_signal(barrier, inc=1, device_id=(tx, ty), device_id_type=MESH)

    every_peer(greet)
    loads = {}
    for n, (name, src, dst) in enumerate((
        ("cell", cell_in, cell_ref), ("guess", guess_in, guess_ref), ("slot", slot_in, slot_ref),
        ("winv", winv_in, winv_ref), ("face", face_in, face_ref), ("win", win_in, win_ref),
        ("wout", wout_in, wout_ref), ("mob", mob_in, mob_ref), ("diag", diag_in, diag_ref),
        ("right", right_in, right_ref), ("colinv", colinv_in, colinv_ref),
    )):
        loads[name] = pltpu.make_async_copy(src, dst, load_sem.at[n])
        loads[name].start()

    sub = lax.broadcasted_iota(jnp.int32, (128, 128), 0)
    lane = lax.broadcasted_iota(jnp.int32, (128, 128), 1)
    sub8 = lax.broadcasted_iota(jnp.int32, (8, 128), 0)

    def send(index):
        def one(tx, ty):
            pltpu.make_async_remote_copy(
                src_ref=snd.at[index, tx * 32 + ty], dst_ref=rcv.at[index, me],
                send_sem=snd_sem.at[index], recv_sem=rcv_sem.at[index],
                device_id=(tx, ty), device_id_type=MESH,
            ).start()

        every_peer(one)
        rcv[index, pl.ds(me, 1), :] = snd[index, pl.ds(me, 1), :]

    def receive(index):
        rows = pl.ds(0, DEV - 1)
        pltpu.make_async_copy(
            snd.at[index, rows], rcv.at[index, rows], rcv_sem.at[index]
        ).wait()
        return rcv[index].T

    def sent(index):
        rows = pl.ds(0, DEV - 1)
        pltpu.make_async_copy(
            snd.at[index, rows], rcv.at[index, rows], snd_sem.at[index]
        ).wait()

    def post(index, dots=()):
        for j, value in enumerate(dots):
            mt[16 + j : 17 + j, :] = jnp.broadcast_to(value, (1, 128))
        snd[index] = mt[...].T
        send(index)

    def lane_sum(received, j):
        return jnp.sum(received[16 + j : 17 + j], axis=1, keepdims=True)

    mt[...] = jnp.zeros((128, 128), F32)
    loads["cell"].wait()
    cells = cell_ref[:, 0, :]
    row_of = lax.shift_right_logical(cells, 7)
    col_of = lax.bitwise_and(cells, 127)
    for q in range(CAP):
        part = slice(q * 128, (q + 1) * 128)
        hot = jnp.where(sub == row_of[q : q + 1], 1.0, 0.0).astype(BF16)
        oht[0:128, part] = hot
        oht[128:256, part] = hot
        col_hot = jnp.where(sub == col_of[q : q + 1], 1.0, 0.0)
        cmt[:, part] = col_hot
        cmb[:, part] = col_hot.astype(BF16)
    vals[...] = jnp.zeros((48, 128), F32)
    def gather(fields):
        stacked = jnp.concatenate([field.T for field in fields], axis=0)
        high, low = split(stacked)
        pair = jnp.concatenate([high.astype(BF16), low.astype(BF16)], axis=1)
        for q in range(0, CAP, 2):
            part = slice(q * 128, (q + 2) * 128)
            picked = dot(pair, oht[:, part])
            mask = cmt[:, part]
            for c in range(3):
                value = jnp.sum(picked[c * 128 : (c + 1) * 128] * mask, axis=0, keepdims=True)
                vals[c * 16 + q : c * 16 + q + 1, :] = value[:, 0:128]
                vals[c * 16 + q + 1 : c * 16 + q + 2, :] = value[:, 128:256]

    def by_slot(rows):
        high, low = split(rows)
        both = jnp.concatenate([high, low], axis=0).astype(BF16)
        spread = dot(both, gt[...])
        count = rows.shape[0]
        spread = spread[0:count] + spread[count:]
        return [
            jnp.sum(spread[n : n + 8] * wmask[...], axis=0, keepdims=True)
            for n in range(0, count, 8)
        ]

    def put_rows(ref, base, row):
        for q in range(CAP):
            ref[base + q : base + q + 1, :] = row[:, q * 128 : (q + 1) * 128]

    def solve_wells(rate):
        spread = jnp.concatenate(
            [jnp.broadcast_to(rate[q : q + 1], (8, 128)) for q in range(CAP)], axis=1
        ) * wmask[...]
        high, low = split(spread)
        totals = dot(jnp.concatenate([high, low], axis=0).astype(BF16), gts[...])
        high, low = split(totals[0:8] + totals[8:16])
        left = jnp.concatenate(
            [
                jnp.concatenate([high, high], axis=1),
                jnp.concatenate([low, jnp.zeros_like(low)], axis=1),
            ],
            axis=0,
        ).astype(BF16)
        product = dot(left, solver[...])
        product = (product[0:8] + product[8:16]) * wmask[...]
        put_rows(mt, 0, jnp.sum(product, axis=0, keepdims=True))

    def scatter(back):
        pieces = [split(coef[3 + c] * back) for c in range(3)]
        for half in range(2):
            for q in range(CAP):
                part = slice(q * 128, (q + 1) * 128)
                into = slice((half * CAP + q) * 128, (half * CAP + q + 1) * 128)
                for c in range(3):
                    row = jnp.broadcast_to(pieces[c][half][q : q + 1], (16, 128)).astype(BF16)
                    spread = jnp.concatenate([row] * 8, axis=0)
                    terms[c * 128 : (c + 1) * 128, into] = cmb[:, part] * spread
        right = terms[...]
        left = jnp.concatenate([oht[0:128], oht[0:128]], axis=1)
        term = dot_nt(left, right)
        return [term[:, c * 128 : (c + 1) * 128] for c in range(3)]

    def couple(ref, fields, a):
        out = flat(ref[:, a, 0].astype(F32)) * fields[0]
        out = out + flat(ref[:, a, 1].astype(F32)) * fields[1]
        return out + flat(ref[:, a, 2].astype(F32)) * fields[2]

    def halo_copies(op):
        low, high = (gx + 3) % 4, (gx + 1) % 4
        left, right = (gy + 31) % 32, (gy + 1) % 32

        def row_copy(mine, theirs, which, target):
            return pltpu.make_async_remote_copy(
                src_ref=flux_pad.at[op, :, :, mine], dst_ref=flux_pad.at[op, :, :, theirs],
                send_sem=hs_sem.at[op, which], recv_sem=hr_sem.at[op, which],
                device_id=(target, gy), device_id_type=MESH,
            )

        def col_copy(which, target):
            return pltpu.make_async_remote_copy(
                src_ref=col_snd.at[op], dst_ref=col_rcv.at[op, which],
                send_sem=hs_sem.at[op, 2 + which], recv_sem=hr_sem.at[op, 2 + which],
                device_id=(gx, target), device_id_type=MESH,
            )

        return (
            row_copy(23, 7, 0, high),
            row_copy(8, 24, 1, low),
            col_copy(0, right),
            col_copy(1, left),
        )

    def stencil_start(op, fields):
        fluxes = [couple(mob_ref, fields, a) for a in range(3)]
        packed = jnp.zeros((128, 128), F32)
        for a in range(3):
            flux_pad[op, a, :, 8:24, :] = fluxes[a].reshape(8, 16, 128)
            packed = jnp.where(lane == a, fluxes[a][:, 127:128], packed)
            packed = jnp.where(lane == 3 + a, fluxes[a][:, 0:1], packed)
        col_snd[op] = packed.T[0:8]
        copies = halo_copies(op)
        for copy in copies:
            copy.start()
        centre = []
        for a in range(3):
            flux = fluxes[a]
            zero = jnp.zeros((16, 128), F32)
            out = couple(diag_ref, fields, a)
            out = out - faces[4] * jnp.concatenate([zero, flux[0:112]], axis=0)
            out = out - faces[5] * jnp.concatenate([flux[16:128], zero], axis=0)
            centre.append(out)
        return copies, centre

    def stencil_end(op, copies, centre):
        for copy in copies:
            copy.wait()
        edge_low = jnp.concatenate([col_rcv[op, 0], jnp.zeros((120, 128), F32)], axis=0).T
        edge_high = jnp.concatenate([col_rcv[op, 1], jnp.zeros((120, 128), F32)], axis=0).T
        outs = []
        for a in range(3):
            flux = flat(flux_pad[op, a, :, 8:24, :])
            before = jnp.where(lane == 0, edge_low[:, a : a + 1], pltpu.roll(flux, 1, 1))
            after = jnp.where(lane == 127, edge_high[:, 3 + a : 4 + a], pltpu.roll(flux, 127, 1))
            out = centre[a] - faces[0] * flat(flux_pad[op, a, :, 7:23, :])
            out = out - faces[1] * flat(flux_pad[op, a, :, 9:25, :])
            out = out - faces[2] * before
            outs.append(out - faces[3] * after)
        return outs

    def precondition(fields):
        paired = [field.reshape(4, 2, 16, 128) for field in fields]
        results = []
        for e in range(6):
            total = None
            for f in range(6):
                term = colinv_ref[:, e, f].astype(F32) * paired[f % 3][:, f // 3]
                total = term if total is None else total + term
            results.append(total)
        return [
            flat(jnp.concatenate([results[c][:, None], results[3 + c][:, None]], axis=1))
            for c in range(3)
        ]

    def combine(scale, xs, ys):
        return [x + scale * y for x, y in zip(xs, ys)]

    loads["guess"].wait()
    guess = [flat(guess_ref[:, c]) for c in range(3)]
    gather(guess)
    mt[0:48, :] = vals[...]
    snd[0] = mt[...].T
    pl.semaphore_wait(barrier, DEV - 1)
    send(0)
    for name in ("win", "wout", "mob", "diag", "right", "colinv"):
        loads[name].wait()
    inner = lax.bitwise_and(sub, 15)
    layer = lax.shift_right_logical(sub, 4)
    outside = (
        (inner == 0) & (gx == 0),
        (inner == 15) & (gx == 3),
        (lane == 0) & (gy == 0),
        (lane == 127) & (gy == 31),
        layer == 0,
        layer == 7,
    )
    loads["face"].wait()
    for n in range(6):
        faces[n] = jnp.where(outside[n], 0.0, flat(face_ref[n].astype(F32)))

    started = stencil_start(0, guess)
    loads["slot"].wait()
    slots = slot_ref[:, 0, :]
    well_of = lax.shift_right_logical(slots, 7)
    seg_of = lax.bitwise_and(slots, 127)
    for q in range(CAP):
        part = slice(q * 128, (q + 1) * 128)
        seg_hot = jnp.where(sub == seg_of[q : q + 1], 1.0, 0.0)
        gt[:, part] = seg_hot.astype(BF16)
        gts[part, :] = seg_hot.T.astype(BF16)
        wmask[:, part] = jnp.where(sub8 == well_of[q : q + 1], 1.0, 0.0)
    loads["winv"].wait()
    fused = None
    for w in range(8):
        high, low = split(winv_ref[w].T)
        rows = dot(high.astype(BF16), gt[...]) + dot(low.astype(BF16), gt[...])
        rows = rows * wmask[w : w + 1, :]
        fused = rows if fused is None else fused + rows
    high, low = split(fused)
    solver[0:128, :] = high.astype(BF16)
    solver[128:256, :] = low.astype(BF16)

    rows = [win_ref[c : c + 1, w * 128 : (w + 1) * 128] for c in range(3) for w in range(8)]
    rows += [wout_ref[c : c + 1, w * 128 : (w + 1) * 128] for c in range(3) for w in range(8)]
    own = by_slot(jnp.concatenate(rows, axis=0))
    mt[...] = jnp.zeros((128, 128), F32)
    for n in range(6):
        put_rows(mt, 16 + n * 16, own[n])
    got = receive(0)
    rate = sum(mt[16 + 16 * c : 32 + 16 * c, :] * got[16 * c : 16 * c + 16] for c in range(3))
    solve_wells(rate)
    post(1)
    applied = stencil_end(0, *started)
    got = receive(1)
    for n in range(6):
        coef[n] = got[16 + 16 * n : 32 + 16 * n]
    term = scatter(got[0:16])
    r0 = [flat(right_ref[:, c]) - (applied[c] - term[c]) for c in range(3)]

    def rates_of(fields):
        gather(fields)
        return coef[0] * vals[0:16] + coef[1] * vals[16:32] + coef[2] * vals[32:48]

    def build_link():
        half = lax.bitwise_and(lax.shift_right_logical(row_of, 4), 1)
        key = lax.bitwise_and(row_of, 15) * 128 + col_of
        key = (key + lax.shift_right_logical(row_of, 5) * 2048).astype(F32)
        weights = []
        for f in range(6):
            stacked = jnp.concatenate(
                [
                    jnp.concatenate(
                        [colinv_ref[:, c, f][:, None], colinv_ref[:, 3 + c, f][:, None]], axis=1
                    ).astype(F32).reshape(128, 128).T
                    for c in range(3)
                ],
                axis=0,
            ).astype(BF16)
            for q in range(0, CAP, 2):
                part = slice(q * 128, (q + 2) * 128)
                picked = dot(stacked, oht[0:128, part])
                total = None
                for c in range(3):
                    row = jnp.concatenate(
                        [coef[c, q : q + 1, :], coef[c, q + 1 : q + 2, :]], axis=1
                    )
                    term = picked[c * 128 : (c + 1) * 128] * row
                    total = term if total is None else total + term
                total = jnp.sum(total * cmt[:, part], axis=0, keepdims=True)
                high, low = split(total)
                link_w[f : f + 1, part] = high
                link_w[6 + f : 7 + f, part] = high
                link_w[12 + f : 13 + f, part] = low
        link_w[18:32, :] = jnp.zeros((14, SLOTS), F32)
        right = link_w[...].astype(BF16)
        keys = jnp.concatenate([key[q : q + 1] for q in range(CAP)], axis=1)
        link_a[...] = jnp.zeros((128, 128), F32)
        for q in range(CAP):
            for f in range(6):
                own = jnp.where(half[q : q + 1] == f // 3, coef[3 + f % 3, q : q + 1, :], 0.0)
                high, low = split(own)
                link_a[f : f + 1, :] = high
                link_a[6 + f : 7 + f, :] = low
                link_a[12 + f : 13 + f, :] = high
            link_a[32:33, :] = key[q : q + 1]
            turned = link_a[...].T
            product = dot(turned[:, 0:32].astype(BF16), right)
            same = jnp.broadcast_to(turned[:, 32:33], (128, SLOTS)) == keys
            link[q * 128 : (q + 1) * 128, :] = jnp.where(same, product, 0.0)

    def linked(index):
        total = jnp.zeros((8, SLOTS), F32)
        for q in range(CAP):
            for n in range(0, 128, 8):
                value = jnp.broadcast_to(rcv[index, n : n + 8, q : q + 1], (8, SLOTS))
                total = total + value * link[q * 128 + n : q * 128 + n + 8, :]
        put_rows(link_out, 0, jnp.sum(total, axis=0, keepdims=True))
        return link_out[...]

    def compact_sum(left, right):
        total = jnp.sum(left * right, axis=0, keepdims=True)
        return jnp.sum(total, axis=1, keepdims=True)

    def minus_wells(applied, back):
        term = scatter(back)
        return [applied[c] - term[c] for c in range(3)]

    link_out[...] = jnp.zeros((16, 128), F32)
    u1 = precondition(r0)
    mt[0:16, :] = rates_of(u1)
    post(2)
    started = stencil_start(1, u1)
    build_link()
    gather(r0)
    r0_out = coef[3] * vals[0:16] + coef[4] * vals[16:32] + coef[5] * vals[32:48]
    own_rho = local_sum(r0, r0)
    solve_wells(receive(2)[0:16])
    post(3, [own_rho])
    d1 = stencil_end(1, *started)
    rates_d = rates_of(precondition(d1))
    own_d = local_sum(r0, d1)
    got = receive(3)
    rho0 = lane_sum(got, 0)
    back = got[0:16]
    rates2 = rates_d - linked(3)
    own_v = own_d - compact_sum(r0_out, back)
    mt[0:16, :] = rates2
    post(4, [own_v])
    v0 = minus_wells(d1, back)
    u2 = precondition(v0)
    started = stencil_start(2, u2)
    got = receive(4)
    alpha0 = rho0 / lane_sum(got, 0)
    solve_wells(got[0:16])
    post(5)
    d2 = stencil_end(2, *started)
    rates_d = rates_of(precondition(d2))
    got = receive(5)
    rates_y = rates_d - linked(5)
    rates3 = rates2 - alpha0 * rates_y
    mt[0:16, :] = rates3
    post(6)
    y0 = minus_wells(d2, got[0:16])
    s0 = combine(-alpha0, r0, v0)
    t0 = combine(-alpha0, v0, y0)
    u3 = precondition(t0)
    started = stencil_start(3, u3)
    own_y = local_sum(r0, y0)
    own_t = local_sum(r0, t0)
    own_dots = [local_sum(t0, s0), local_sum(t0, t0), local_sum(r0, s0), own_t]
    solve_wells(receive(6)[0:16])
    post(7, own_dots)
    d3 = stencil_end(3, *started)
    rates_d = rates_of(precondition(d3))
    own_d = local_sum(r0, d3)
    got = receive(7)
    omega0 = lane_sum(got, 0) / lane_sum(got, 1)
    rho1 = lane_sum(got, 2) - omega0 * lane_sum(got, 3)
    beta = rho1 / rho0 * (alpha0 / omega0)
    back = got[0:16]
    rates_w = rates_d - linked(7)
    mt[0:16, :] = rates3 - omega0 * rates_w + beta * (rates2 - omega0 * rates_y)
    own_w = own_d - compact_sum(r0_out, back)
    post(8, [own_t - omega0 * own_w + beta * (own_v - omega0 * own_y)])
    w0 = minus_wells(d3, back)
    r1 = combine(-omega0, s0, t0)
    a_r1 = combine(-omega0, t0, w0)
    v1 = combine(beta, a_r1, combine(-omega0, v0, y0))
    u4 = precondition(v1)
    started = stencil_start(4, u4)
    got = receive(8)
    alpha1 = rho1 / lane_sum(got, 0)
    solve_wells(got[0:16])
    post(9)
    d4 = stencil_end(4, *started)
    s1 = combine(-alpha1, r1, v1)
    got = receive(9)
    t1 = combine(-alpha1, a_r1, minus_wells(d4, got[0:16]))
    post(10, [local_sum(t1, s1), local_sum(t1, t1)])
    ms0 = combine(-alpha0, u1, u2)
    mr1 = combine(-omega0, ms0, u3)
    mp1 = combine(beta, mr1, combine(-omega0, u1, u2))
    ms1 = combine(-alpha1, mr1, u4)
    guess = [flat(guess_ref[:, c]) for c in range(3)]
    partial = combine(alpha1, combine(omega0, combine(alpha0, guess, u1), ms0), mp1)
    got = receive(10)
    omega1 = lane_sum(got, 0) / lane_sum(got, 1)
    final = combine(omega1, partial, ms1)
    left = combine(-omega1, s1, t1)
    for c in range(3):
        sol_ref[:, c] = final[c].reshape(8, 16, 128)
        res_ref[:, c] = left[c].reshape(8, 16, 128)
    for index in range(EXCHANGES):
        sent(index)


def per_device(*args):
    args = list(args)
    for n in (6, 7):
        args[n] = jnp.transpose(args[n], (2, 0, 1))
    shape = args[0].shape
    hbm = pl.BlockSpec(memory_space=pltpu.HBM)
    vmem = pl.BlockSpec(memory_space=pltpu.VMEM)
    return pl.pallas_call(
        kernel,
        out_shape=(jax.ShapeDtypeStruct(shape, F32), jax.ShapeDtypeStruct(shape, F32)),
        in_specs=[hbm] * 11,
        out_specs=(vmem, vmem),
        scratch_shapes=[pltpu.VMEM(arg.shape, arg.dtype) for arg in args]
        + [
            pltpu.SemaphoreType.DMA((11,)),
            pltpu.VMEM((EXCHANGES, 128, 128), F32),
            pltpu.VMEM((EXCHANGES, 128, 128), F32),
            pltpu.VMEM((OPS, 3, 8, 32, 128), F32),
            pltpu.VMEM((OPS, 8, 128), F32),
            pltpu.VMEM((OPS, 2, 8, 128), F32),
            pltpu.VMEM((128, 128), F32),
            pltpu.VMEM((6, 128, 128), F32),
            pltpu.VMEM((256, SLOTS), BF16),
            pltpu.VMEM((128, SLOTS), F32),
            pltpu.VMEM((128, SLOTS), BF16),
            pltpu.VMEM((384, 2 * SLOTS), BF16),
            pltpu.VMEM((SLOTS, 128), BF16),
            pltpu.VMEM((128, SLOTS), BF16),
            pltpu.VMEM((8, SLOTS), F32),
            pltpu.VMEM((256, SLOTS), BF16),
            pltpu.VMEM((48, 128), F32),
            pltpu.VMEM((6, 16, 128), F32),
            pltpu.VMEM((SLOTS, SLOTS), F32),
            pltpu.VMEM((32, SLOTS), F32),
            pltpu.VMEM((128, 128), F32),
            pltpu.VMEM((16, 128), F32),
            pltpu.SemaphoreType.DMA((EXCHANGES,)),
            pltpu.SemaphoreType.DMA((EXCHANGES,)),
            pltpu.SemaphoreType.DMA((OPS, 4)),
            pltpu.SemaphoreType.DMA((OPS, 4)),
        ],
        compiler_params=pltpu.CompilerParams(
            collective_id=0, has_side_effects=True, vmem_limit_bytes=60 * 1024 * 1024
        ),
    )(*args)


def solution(mesh):
    in_specs = (
        P(None, None, "gx", "gy"),
        P(None, None, "gx", "gy"),
        P(None, None, None, "gx", "gy"),
        P(None, None, None, "gx", "gy"),
        P(None, None, "gx", "gy"),
        P(None, None, None, "gx", "gy"),
        P(("gx", "gy"), None, None),
        P(("gx", "gy"), None, None),
        P(None, ("gx", "gy")),
        P(None, ("gx", "gy")),
        P(("gx", "gy"), None, None),
    )
    out_specs = (P(None, None, "gx", "gy"), P(None, None, "gx", "gy"))
    return jax.shard_map(
        per_device, mesh=mesh, in_specs=in_specs, out_specs=out_specs, check_vma=False
    )
```

```python
import jax
import jax.numpy as jnp
from jax import lax
from jax.experimental import pallas as pl
from jax.experimental.pallas import tpu as pltpu
from jax.sharding import PartitionSpec as P

MESH = pl.DeviceIdType.MESH
F32 = jnp.float32
BF16 = jnp.bfloat16
DEV = 128
CAP = 10
FAR_FIRST = (2, 3, 1, 0)
SLOTS = DEV * CAP
OPS = 5
EXCHANGES = 2 * OPS + 1


def dot(a, b):
    return lax.dot_general(a, b, (((1,), (0,)), ((), ())), preferred_element_type=F32)


def dot_nt(a, b):
    return lax.dot_general(a, b, (((1,), (1,)), ((), ())), preferred_element_type=F32)


def split(value):
    high = value.astype(BF16).astype(F32)
    return high, value - high


def flat(value):
    return value.reshape(128, 128)


def local_sum(lefts, rights):
    total = lefts[0] * rights[0] + lefts[1] * rights[1] + lefts[2] * rights[2]
    return jnp.sum(jnp.sum(total, axis=0, keepdims=True), axis=1, keepdims=True)


def kernel(
    right_in, guess_in, diag_in, mob_in, face_in, colinv_in, cell_in, slot_in, win_in, wout_in,
    winv_in, sol_ref, res_ref,
    right_ref, guess_ref, diag_ref, mob_ref, face_ref, colinv_ref, cell_ref, slot_ref, win_ref,
    wout_ref, winv_ref, load_sem,
    snd, rcv, flux_pad, col_snd, col_rcv, mt, faces, oht, cmt, cmb, terms, gts, gt, wmask, solver, vals, coef, link,
    link_w, link_a, link_out, own_in,
    snd_sem, rcv_sem, hs_sem, hr_sem,
):
    gx = lax.axis_index("gx")
    gy = lax.axis_index("gy")
    me = gx * 32 + gy
    pz, py, pc = lax.div(gy, 8), lax.rem(lax.div(gy, 2), 4), lax.rem(gy, 2)
    near = [
        (oy, oc, lax.rem(py + oy, 4) * 2 + (1 - pc if oc else pc)) for oy in FAR_FIRST for oc in (1, 0)
    ]

    xs = [lax.rem(gx + o, 4) for o in range(4)]
    zs = [lax.rem(pz + o, 4) * 8 for o in range(4)]

    def every_peer(act):
        for ox in FAR_FIRST:
            for oz in FAR_FIRST:
                for oy, oc, low in near:
                    if ox or oz or oy or oc:
                        act(xs[ox], zs[oz] + low)

    barrier = pltpu.get_barrier_semaphore()

    def greet(tx, ty):
        pl.semaphore_signal(barrier, inc=1, device_id=(tx, ty), device_id_type=MESH)

    every_peer(greet)
    loads = {}
    for n, (name, src, dst) in enumerate((
        ("cell", cell_in, cell_ref), ("guess", guess_in, guess_ref), ("slot", slot_in, slot_ref),
        ("winv", winv_in, winv_ref), ("face", face_in, face_ref), ("win", win_in, win_ref),
        ("wout", wout_in, wout_ref), ("mob", mob_in, mob_ref), ("diag", diag_in, diag_ref),
        ("right", right_in, right_ref), ("colinv", colinv_in, colinv_ref),
    )):
        loads[name] = pltpu.make_async_copy(src, dst, load_sem.at[n])
        loads[name].start()

    sub = lax.broadcasted_iota(jnp.int32, (128, 128), 0)
    lane = lax.broadcasted_iota(jnp.int32, (128, 128), 1)
    sub8 = lax.broadcasted_iota(jnp.int32, (8, 128), 0)

    def send(index):
        def one(tx, ty):
            pltpu.make_async_remote_copy(
                src_ref=snd.at[index, tx * 32 + ty], dst_ref=rcv.at[index, me],
                send_sem=snd_sem.at[index], recv_sem=rcv_sem.at[index],
                device_id=(tx, ty), device_id_type=MESH,
            ).start()

        every_peer(one)
        rcv[index, pl.ds(me, 1), :] = snd[index, pl.ds(me, 1), :]

    def receive_wide(index):
        rows = pl.ds(0, DEV - 1)
        pltpu.make_async_copy(
            snd.at[index, rows], rcv.at[index, rows], rcv_sem.at[index]
        ).wait()
        return rcv[index].T

    def receive(index):
        return receive_wide(index)

    def sent(index):
        rows = pl.ds(0, DEV - 1)
        pltpu.make_async_copy(
            snd.at[index, rows], rcv.at[index, rows], snd_sem.at[index]
        ).wait()

    def post(index, dots=()):
        for j, value in enumerate(dots):
            mt[16 + j : 17 + j, :] = jnp.broadcast_to(value, (1, 128))
        snd[index] = mt[...].T
        send(index)

    def lane_sum(received, j):
        return jnp.sum(received[16 + j : 17 + j], axis=1, keepdims=True)

    mt[...] = jnp.zeros((128, 128), F32)
    loads["cell"].wait()
    cells = cell_ref[:, 0, :]
    row_of = lax.shift_right_logical(cells, 7)
    col_of = lax.bitwise_and(cells, 127)
    for q in range(CAP):
        part = slice(q * 128, (q + 1) * 128)
        hot = jnp.where(sub == row_of[q : q + 1], 1.0, 0.0).astype(BF16)
        oht[0:128, part] = hot
        oht[128:256, part] = hot
        col_hot = jnp.where(sub == col_of[q : q + 1], 1.0, 0.0)
        cmt[:, part] = col_hot
        cmb[:, part] = col_hot.astype(BF16)
    vals[...] = jnp.zeros((48, 128), F32)
    def gather(fields):
        stacked = jnp.concatenate([field.T for field in fields], axis=0)
        high, low = split(stacked)
        pair = jnp.concatenate([high.astype(BF16), low.astype(BF16)], axis=1)
        for q in range(0, CAP, 2):
            part = slice(q * 128, (q + 2) * 128)
            picked = dot(pair, oht[:, part])
            mask = cmt[:, part]
            for c in range(3):
                value = jnp.sum(picked[c * 128 : (c + 1) * 128] * mask, axis=0, keepdims=True)
                vals[c * 16 + q : c * 16 + q + 1, :] = value[:, 0:128]
                vals[c * 16 + q + 1 : c * 16 + q + 2, :] = value[:, 128:256]

    def by_slot(rows):
        high, low = split(rows)
        both = jnp.concatenate([high, low], axis=0).astype(BF16)
        spread = dot(both, gt[...])
        count = rows.shape[0]
        spread = spread[0:count] + spread[count:]
        return [
            jnp.sum(spread[n : n + 8] * wmask[...], axis=0, keepdims=True)
            for n in range(0, count, 8)
        ]

    def put_rows(ref, base, row):
        for q in range(CAP):
            ref[base + q : base + q + 1, :] = row[:, q * 128 : (q + 1) * 128]

    def solve_wells(rate):
        spread = jnp.concatenate(
            [jnp.broadcast_to(rate[q : q + 1], (8, 128)) for q in range(CAP)], axis=1
        ) * wmask[...]
        high, low = split(spread)
        totals = dot(jnp.concatenate([high, low], axis=0).astype(BF16), gts[...])
        high, low = split(totals[0:8] + totals[8:16])
        left = jnp.concatenate(
            [
                jnp.concatenate([high, high], axis=1),
                jnp.concatenate([low, jnp.zeros_like(low)], axis=1),
            ],
            axis=0,
        ).astype(BF16)
        product = dot(left, solver[...])
        product = (product[0:8] + product[8:16]) * wmask[...]
        put_rows(mt, 0, jnp.sum(product, axis=0, keepdims=True))

    def scatter(back):
        pieces = [split(coef[3 + c] * back) for c in range(3)]
        for half in range(2):
            for q in range(CAP):
                part = slice(q * 128, (q + 1) * 128)
                into = slice((half * CAP + q) * 128, (half * CAP + q + 1) * 128)
                for c in range(3):
                    row = jnp.broadcast_to(pieces[c][half][q : q + 1], (16, 128)).astype(BF16)
                    spread = jnp.concatenate([row] * 8, axis=0)
                    terms[c * 128 : (c + 1) * 128, into] = cmb[:, part] * spread
        right = terms[...]
        left = jnp.concatenate([oht[0:128], oht[0:128]], axis=1)
        term = dot_nt(left, right)
        return [term[:, c * 128 : (c + 1) * 128] for c in range(3)]

    def couple(ref, fields, a):
        out = flat(ref[:, a, 0].astype(F32)) * fields[0]
        out = out + flat(ref[:, a, 1].astype(F32)) * fields[1]
        return out + flat(ref[:, a, 2].astype(F32)) * fields[2]

    def halo_copies(op):
        low, high = (gx + 3) % 4, (gx + 1) % 4
        left, right = (gy + 31) % 32, (gy + 1) % 32

        def row_copy(mine, theirs, which, target):
            return pltpu.make_async_remote_copy(
                src_ref=flux_pad.at[op, :, :, mine], dst_ref=flux_pad.at[op, :, :, theirs],
                send_sem=hs_sem.at[op, which], recv_sem=hr_sem.at[op, which],
                device_id=(target, gy), device_id_type=MESH,
            )

        def col_copy(which, target):
            return pltpu.make_async_remote_copy(
                src_ref=col_snd.at[op], dst_ref=col_rcv.at[op, which],
                send_sem=hs_sem.at[op, 2 + which], recv_sem=hr_sem.at[op, 2 + which],
                device_id=(gx, target), device_id_type=MESH,
            )

        return (
            row_copy(23, 7, 0, high),
            row_copy(8, 24, 1, low),
            col_copy(0, right),
            col_copy(1, left),
        )

    def stencil_start(op, fields):
        fluxes = [couple(mob_ref, fields, a) for a in range(3)]
        packed = jnp.zeros((128, 128), F32)
        for a in range(3):
            flux_pad[op, a, :, 8:24, :] = fluxes[a].reshape(8, 16, 128)
            packed = jnp.where(lane == a, fluxes[a][:, 127:128], packed)
            packed = jnp.where(lane == 3 + a, fluxes[a][:, 0:1], packed)
        col_snd[op] = packed.T[0:8]
        copies = halo_copies(op)
        for copy in copies:
            copy.start()
        centre = []
        for a in range(3):
            flux = fluxes[a]
            zero = jnp.zeros((16, 128), F32)
            out = couple(diag_ref, fields, a)
            out = out - faces[4] * jnp.concatenate([zero, flux[0:112]], axis=0)
            out = out - faces[5] * jnp.concatenate([flux[16:128], zero], axis=0)
            centre.append(out)
        return copies, centre

    def stencil_end(op, copies, centre):
        for copy in copies:
            copy.wait()
        edge_low = jnp.concatenate([col_rcv[op, 0], jnp.zeros((120, 128), F32)], axis=0).T
        edge_high = jnp.concatenate([col_rcv[op, 1], jnp.zeros((120, 128), F32)], axis=0).T
        outs = []
        for a in range(3):
            flux = flat(flux_pad[op, a, :, 8:24, :])
            before = jnp.where(lane == 0, edge_low[:, a : a + 1], pltpu.roll(flux, 1, 1))
            after = jnp.where(lane == 127, edge_high[:, 3 + a : 4 + a], pltpu.roll(flux, 127, 1))
            out = centre[a] - faces[0] * flat(flux_pad[op, a, :, 7:23, :])
            out = out - faces[1] * flat(flux_pad[op, a, :, 9:25, :])
            out = out - faces[2] * before
            outs.append(out - faces[3] * after)
        return outs

    def precondition(fields):
        paired = [field.reshape(4, 2, 16, 128) for field in fields]
        results = []
        for e in range(6):
            total = None
            for f in range(6):
                term = colinv_ref[:, e, f].astype(F32) * paired[f % 3][:, f // 3]
                total = term if total is None else total + term
            results.append(total)
        return [
            flat(jnp.concatenate([results[c][:, None], results[3 + c][:, None]], axis=1))
            for c in range(3)
        ]

    def combine(scale, xs, ys):
        return [x + scale * y for x, y in zip(xs, ys)]

    def rates_of(fields):
        gather(fields)
        return coef[0] * vals[0:16] + coef[1] * vals[16:32] + coef[2] * vals[32:48]

    def build_link():
        half = lax.bitwise_and(lax.shift_right_logical(row_of, 4), 1)
        key = lax.bitwise_and(row_of, 15) * 128 + col_of
        key = (key + lax.shift_right_logical(row_of, 5) * 2048).astype(F32)
        weights = []
        for f in range(6):
            stacked = jnp.concatenate(
                [
                    jnp.concatenate(
                        [colinv_ref[:, c, f][:, None], colinv_ref[:, 3 + c, f][:, None]], axis=1
                    ).astype(F32).reshape(128, 128).T
                    for c in range(3)
                ],
                axis=0,
            ).astype(BF16)
            for q in range(0, CAP, 2):
                part = slice(q * 128, (q + 2) * 128)
                picked = dot(stacked, oht[0:128, part])
                total = None
                for c in range(3):
                    row = jnp.concatenate(
                        [coef[c, q : q + 1, :], coef[c, q + 1 : q + 2, :]], axis=1
                    )
                    term = picked[c * 128 : (c + 1) * 128] * row
                    total = term if total is None else total + term
                total = jnp.sum(total * cmt[:, part], axis=0, keepdims=True)
                high, low = split(total)
                link_w[f : f + 1, part] = high
                link_w[6 + f : 7 + f, part] = high
                link_w[12 + f : 13 + f, part] = low
        link_w[18:32, :] = jnp.zeros((14, SLOTS), F32)
        right = link_w[...].astype(BF16)
        keys = jnp.concatenate([key[q : q + 1] for q in range(CAP)], axis=1)
        link_a[...] = jnp.zeros((128, 128), F32)
        for q in range(CAP):
            for f in range(6):
                own = jnp.where(half[q : q + 1] == f // 3, coef[3 + f % 3, q : q + 1, :], 0.0)
                high, low = split(own)
                link_a[f : f + 1, :] = high
                link_a[6 + f : 7 + f, :] = low
                link_a[12 + f : 13 + f, :] = high
            link_a[32:33, :] = key[q : q + 1]
            turned = link_a[...].T
            product = dot(turned[:, 0:32].astype(BF16), right)
            same = jnp.broadcast_to(turned[:, 32:33], (128, SLOTS)) == keys
            link[q * 128 : (q + 1) * 128, :] = jnp.where(same, product, 0.0)

    def linked(index):
        total = jnp.zeros((8, SLOTS), F32)
        for q in range(CAP):
            for n in range(0, 128, 8):
                value = jnp.broadcast_to(rcv[index, n : n + 8, q : q + 1], (8, SLOTS))
                total = total + value * link[q * 128 + n : q * 128 + n + 8, :]
        put_rows(link_out, 0, jnp.sum(total, axis=0, keepdims=True))
        return link_out[...]

    def compact_sum(left, right):
        total = jnp.sum(left * right, axis=0, keepdims=True)
        return jnp.sum(total, axis=1, keepdims=True)

    def minus_wells(applied, back):
        term = scatter(back)
        return [applied[c] - term[c] for c in range(3)]

    loads["guess"].wait()
    guess = [flat(guess_ref[:, c]) for c in range(3)]
    gather(guess)
    for c in range(3):
        mt[CAP * c : CAP * (c + 1), :] = vals[16 * c : 16 * c + CAP]
    loads["slot"].wait()
    slots = slot_ref[:, 0, :]
    well_of = lax.shift_right_logical(slots, 7)
    seg_of = lax.bitwise_and(slots, 127)
    for q in range(CAP):
        part = slice(q * 128, (q + 1) * 128)
        seg_hot = jnp.where(sub == seg_of[q : q + 1], 1.0, 0.0)
        gt[:, part] = seg_hot.astype(BF16)
        gts[part, :] = seg_hot.T.astype(BF16)
        wmask[:, part] = jnp.where(sub8 == well_of[q : q + 1], 1.0, 0.0)
    for name in ("win", "wout"):
        loads[name].wait()
    rows = [ref[c : c + 1, w * 128 : (w + 1) * 128] for ref in (win_ref, wout_ref) for c in range(3) for w in range(8)]
    own = by_slot(jnp.concatenate(rows, axis=0))
    for n in range(6):
        put_rows(mt, (3 + n) * CAP, own[n])
    for c in range(3):
        put_rows(own_in, c * 16, own[c])
    snd[0] = mt[...].T
    pl.semaphore_wait(barrier, DEV - 1)
    send(0)
    for name in ("mob", "diag", "right", "colinv"):
        loads[name].wait()
    inner = lax.bitwise_and(sub, 15)
    layer = lax.shift_right_logical(sub, 4)
    outside = (
        (inner == 0) & (gx == 0),
        (inner == 15) & (gx == 3),
        (lane == 0) & (gy == 0),
        (lane == 127) & (gy == 31),
        layer == 0,
        layer == 7,
    )
    loads["face"].wait()
    for n in range(6):
        faces[n] = jnp.where(outside[n], 0.0, flat(face_ref[n].astype(F32)))

    started = stencil_start(0, guess)
    loads["winv"].wait()
    fused = None
    for w in range(8):
        high, low = split(winv_ref[w].T)
        rows = dot(high.astype(BF16), gt[...]) + dot(low.astype(BF16), gt[...])
        rows = rows * wmask[w : w + 1, :]
        fused = rows if fused is None else fused + rows
    high, low = split(fused)
    solver[0:128, :] = high.astype(BF16)
    solver[128:256, :] = low.astype(BF16)

    coef[...] = jnp.zeros((6, 16, 128), F32)
    link_out[...] = jnp.zeros((16, 128), F32)
    got = receive_wide(0)
    mt[...] = jnp.zeros((128, 128), F32)
    solve_wells(sum(own_in[16 * c : 16 * c + CAP, :] * got[CAP * c : CAP * (c + 1)] for c in range(3)))
    post(1)
    for n in range(6):
        coef[n, 0:CAP, :] = got[(3 + n) * CAP : (4 + n) * CAP]

    applied = stencil_end(0, *started)
    part0 = [flat(right_ref[:, c]) - applied[c] for c in range(3)]
    rates_d = rates_of(precondition(part0))
    build_link()
    got = receive(1)
    mt[0:16, :] = rates_d + linked(1)
    post(2)
    term = scatter(got[0:16])
    r0 = [part0[c] + term[c] for c in range(3)]
    u1 = precondition(r0)
    started = stencil_start(1, u1)
    gather(r0)
    r0_out = coef[3] * vals[0:16] + coef[4] * vals[16:32] + coef[5] * vals[32:48]
    own_rho = local_sum(r0, r0)
    solve_wells(receive(2)[0:16])
    post(3, [own_rho])
    d1 = stencil_end(1, *started)
    rates_d = rates_of(precondition(d1))
    own_d = local_sum(r0, d1)
    got = receive(3)
    rho0 = lane_sum(got, 0)
    back = got[0:16]
    rates2 = rates_d - linked(3)
    own_v = own_d - compact_sum(r0_out, back)
    mt[0:16, :] = rates2
    post(4, [own_v])
    v0 = minus_wells(d1, back)
    u2 = precondition(v0)
    started = stencil_start(2, u2)
    got = receive(4)
    alpha0 = rho0 / lane_sum(got, 0)
    solve_wells(got[0:16])
    post(5)
    d2 = stencil_end(2, *started)
    rates_d = rates_of(precondition(d2))
    got = receive(5)
    rates_y = rates_d - linked(5)
    rates3 = rates2 - alpha0 * rates_y
    mt[0:16, :] = rates3
    post(6)
    y0 = minus_wells(d2, got[0:16])
    s0 = combine(-alpha0, r0, v0)
    t0 = combine(-alpha0, v0, y0)
    u3 = precondition(t0)
    started = stencil_start(3, u3)
    own_y = local_sum(r0, y0)
    own_t = local_sum(r0, t0)
    own_dots = [local_sum(t0, s0), local_sum(t0, t0), local_sum(r0, s0), own_t]
    solve_wells(receive(6)[0:16])
    post(7, own_dots)
    d3 = stencil_end(3, *started)
    rates_d = rates_of(precondition(d3))
    own_d = local_sum(r0, d3)
    got = receive(7)
    omega0 = lane_sum(got, 0) / lane_sum(got, 1)
    rho1 = lane_sum(got, 2) - omega0 * lane_sum(got, 3)
    beta = rho1 / rho0 * (alpha0 / omega0)
    back = got[0:16]
    rates_w = rates_d - linked(7)
    mt[0:16, :] = rates3 - omega0 * rates_w + beta * (rates2 - omega0 * rates_y)
    own_w = own_d - compact_sum(r0_out, back)
    post(8, [own_t - omega0 * own_w + beta * (own_v - omega0 * own_y)])
    w0 = minus_wells(d3, back)
    r1 = combine(-omega0, s0, t0)
    a_r1 = combine(-omega0, t0, w0)
    v1 = combine(beta, a_r1, combine(-omega0, v0, y0))
    u4 = precondition(v1)
    started = stencil_start(4, u4)
    got = receive(8)
    alpha1 = rho1 / lane_sum(got, 0)
    solve_wells(got[0:16])
    post(9)
    d4 = stencil_end(4, *started)
    s1 = combine(-alpha1, r1, v1)
    got = receive(9)
    t1 = combine(-alpha1, a_r1, minus_wells(d4, got[0:16]))
    post(10, [local_sum(t1, s1), local_sum(t1, t1)])
    ms0 = combine(-alpha0, u1, u2)
    mr1 = combine(-omega0, ms0, u3)
    mp1 = combine(beta, mr1, combine(-omega0, u1, u2))
    ms1 = combine(-alpha1, mr1, u4)
    guess = [flat(guess_ref[:, c]) for c in range(3)]
    partial = combine(alpha1, combine(omega0, combine(alpha0, guess, u1), ms0), mp1)
    got = receive(10)
    omega1 = lane_sum(got, 0) / lane_sum(got, 1)
    final = combine(omega1, partial, ms1)
    left = combine(-omega1, s1, t1)
    for c in range(3):
        sol_ref[:, c] = final[c].reshape(8, 16, 128)
        res_ref[:, c] = left[c].reshape(8, 16, 128)
    for index in range(EXCHANGES):
        sent(index)


def per_device(*args):
    args = list(args)
    for n in (6, 7):
        args[n] = jnp.transpose(args[n], (2, 0, 1))
    shape = args[0].shape
    hbm = pl.BlockSpec(memory_space=pltpu.HBM)
    vmem = pl.BlockSpec(memory_space=pltpu.VMEM)
    return pl.pallas_call(
        kernel,
        out_shape=(jax.ShapeDtypeStruct(shape, F32), jax.ShapeDtypeStruct(shape, F32)),
        in_specs=[hbm] * 11,
        out_specs=(vmem, vmem),
        scratch_shapes=[pltpu.VMEM(arg.shape, arg.dtype) for arg in args]
        + [
            pltpu.SemaphoreType.DMA((11,)),
            pltpu.VMEM((EXCHANGES, 128, 128), F32),
            pltpu.VMEM((EXCHANGES, 128, 128), F32),
            pltpu.VMEM((OPS, 3, 8, 32, 128), F32),
            pltpu.VMEM((OPS, 8, 128), F32),
            pltpu.VMEM((OPS, 2, 8, 128), F32),
            pltpu.VMEM((128, 128), F32),
            pltpu.VMEM((6, 128, 128), F32),
            pltpu.VMEM((256, SLOTS), BF16),
            pltpu.VMEM((128, SLOTS), F32),
            pltpu.VMEM((128, SLOTS), BF16),
            pltpu.VMEM((384, 2 * SLOTS), BF16),
            pltpu.VMEM((SLOTS, 128), BF16),
            pltpu.VMEM((128, SLOTS), BF16),
            pltpu.VMEM((8, SLOTS), F32),
            pltpu.VMEM((256, SLOTS), BF16),
            pltpu.VMEM((48, 128), F32),
            pltpu.VMEM((6, 16, 128), F32),
            pltpu.VMEM((SLOTS, SLOTS), F32),
            pltpu.VMEM((32, SLOTS), F32),
            pltpu.VMEM((128, 128), F32),
            pltpu.VMEM((16, 128), F32),
            pltpu.VMEM((48, 128), F32),
            pltpu.SemaphoreType.DMA((EXCHANGES,)),
            pltpu.SemaphoreType.DMA((EXCHANGES,)),
            pltpu.SemaphoreType.DMA((OPS, 4)),
            pltpu.SemaphoreType.DMA((OPS, 4)),
        ],
        compiler_params=pltpu.CompilerParams(
            collective_id=0, has_side_effects=True, vmem_limit_bytes=60 * 1024 * 1024
        ),
    )(*args)


def solution(mesh):
    in_specs = (
        P(None, None, "gx", "gy"),
        P(None, None, "gx", "gy"),
        P(None, None, None, "gx", "gy"),
        P(None, None, None, "gx", "gy"),
        P(None, None, "gx", "gy"),
        P(None, None, None, "gx", "gy"),
        P(("gx", "gy"), None, None),
        P(("gx", "gy"), None, None),
        P(None, ("gx", "gy")),
        P(None, ("gx", "gy")),
        P(("gx", "gy"), None, None),
    )
    out_specs = (P(None, None, "gx", "gy"), P(None, None, "gx", "gy"))
    return jax.shard_map(
        per_device, mesh=mesh, in_specs=in_specs, out_specs=out_specs, check_vma=False
    )
```

```python
import jax
import jax.numpy as jnp
from jax import lax
from jax.experimental import pallas as pl
from jax.experimental.pallas import tpu as pltpu
from jax.sharding import PartitionSpec as P

MESH = pl.DeviceIdType.MESH
F32 = jnp.float32
BF16 = jnp.bfloat16
DEV = 128
CAP = 10
FAR_FIRST = (2, 3, 1, 0)
SLOTS = DEV * CAP
OPS = 5
EXCHANGES = 2 * OPS + 1


def dot(a, b):
    return lax.dot_general(a, b, (((1,), (0,)), ((), ())), preferred_element_type=F32)


def dot_nt(a, b):
    return lax.dot_general(a, b, (((1,), (1,)), ((), ())), preferred_element_type=F32)


def split(value):
    high = value.astype(BF16).astype(F32)
    return high, value - high


def flat(value):
    return value.reshape(128, 128)


def local_sum(lefts, rights):
    total = lefts[0] * rights[0] + lefts[1] * rights[1] + lefts[2] * rights[2]
    return jnp.sum(jnp.sum(total, axis=0, keepdims=True), axis=1, keepdims=True)


def kernel(
    right_in, guess_in, diag_in, mob_in, face_in, colinv_in, cell_in, slot_in, win_in, wout_in,
    winv_in, sol_ref, res_ref,
    right_ref, guess_ref, diag_ref, mob_ref, face_ref, colinv_ref, cell_ref, slot_ref, win_ref,
    wout_ref, winv_ref, load_sem,
    snd, rcv, flux_pad, col_snd, col_rcv, mt, faces, oht, cmt, cmb, terms, gts, gt, wmask, solver, vals, coef, link,
    link_w, link_a, link_out, own_in,
    snd_sem, rcv_sem, hs_sem, hr_sem,
):
    gx = lax.axis_index("gx")
    gy = lax.axis_index("gy")
    me = gx * 32 + gy
    pz, py, pc = lax.div(gy, 8), lax.rem(lax.div(gy, 2), 4), lax.rem(gy, 2)
    near = [
        (oy, oc, lax.rem(py + oy, 4) * 2 + (1 - pc if oc else pc)) for oy in FAR_FIRST for oc in (1, 0)
    ]

    xs = [lax.rem(gx + o, 4) for o in range(4)]
    zs = [lax.rem(pz + o, 4) * 8 for o in range(4)]

    def every_peer(act):
        for ox in FAR_FIRST:
            for oz in FAR_FIRST:
                for oy, oc, low in near:
                    if ox or oz or oy or oc:
                        act(xs[ox], zs[oz] + low)

    barrier = pltpu.get_barrier_semaphore()

    def greet(tx, ty):
        pl.semaphore_signal(barrier, inc=1, device_id=(tx, ty), device_id_type=MESH)

    every_peer(greet)
    loads = {}
    for n, (name, src, dst) in enumerate((
        ("cell", cell_in, cell_ref), ("guess", guess_in, guess_ref), ("slot", slot_in, slot_ref),
        ("winv", winv_in, winv_ref), ("face", face_in, face_ref), ("win", win_in, win_ref),
        ("wout", wout_in, wout_ref), ("mob", mob_in, mob_ref), ("diag", diag_in, diag_ref),
        ("right", right_in, right_ref), ("colinv", colinv_in, colinv_ref),
    )):
        loads[name] = pltpu.make_async_copy(src, dst, load_sem.at[n])
        loads[name].start()

    sub = lax.broadcasted_iota(jnp.int32, (128, 128), 0)
    lane = lax.broadcasted_iota(jnp.int32, (128, 128), 1)
    sub8 = lax.broadcasted_iota(jnp.int32, (8, 128), 0)

    def send(index):
        def one(tx, ty):
            pltpu.make_async_remote_copy(
                src_ref=snd.at[index, tx * 32 + ty], dst_ref=rcv.at[index, me],
                send_sem=snd_sem.at[index], recv_sem=rcv_sem.at[index],
                device_id=(tx, ty), device_id_type=MESH,
            ).start()

        every_peer(one)
        rcv[index, pl.ds(me, 1), :] = snd[index, pl.ds(me, 1), :]

    def arrive(index):
        rows = pl.ds(0, DEV - 1)
        pltpu.make_async_copy(
            snd.at[index, rows], rcv.at[index, rows], rcv_sem.at[index]
        ).wait()

    def receive(index):
        arrive(index)
        return rcv[index].T

    def sent(index):
        rows = pl.ds(0, DEV - 1)
        pltpu.make_async_copy(
            snd.at[index, rows], rcv.at[index, rows], snd_sem.at[index]
        ).wait()

    def post(index, dots=()):
        for j, value in enumerate(dots):
            mt[16 + j : 17 + j, :] = jnp.broadcast_to(value, (1, 128))
        snd[index] = mt[...].T
        send(index)

    def lane_sum(received, j):
        return jnp.sum(received[16 + j : 17 + j], axis=1, keepdims=True)

    mt[...] = jnp.zeros((128, 128), F32)
    loads["cell"].wait()
    cells = cell_ref[:, 0, :]
    row_of = lax.shift_right_logical(cells, 7)
    col_of = lax.bitwise_and(cells, 127)
    for q in range(CAP):
        part = slice(q * 128, (q + 1) * 128)
        hot = jnp.where(sub == row_of[q : q + 1], 1.0, 0.0).astype(BF16)
        oht[0:128, part] = hot
        oht[128:256, part] = hot
        col_hot = jnp.where(sub == col_of[q : q + 1], 1.0, 0.0)
        cmt[:, part] = col_hot
        cmb[:, part] = col_hot.astype(BF16)
    vals[...] = jnp.zeros((48, 128), F32)
    def gather(fields):
        stacked = jnp.concatenate([field.T for field in fields], axis=0)
        high, low = split(stacked)
        pair = jnp.concatenate([high.astype(BF16), low.astype(BF16)], axis=1)
        for q in range(0, CAP, 2):
            part = slice(q * 128, (q + 2) * 128)
            picked = dot(pair, oht[:, part])
            mask = cmt[:, part]
            for c in range(3):
                value = jnp.sum(picked[c * 128 : (c + 1) * 128] * mask, axis=0, keepdims=True)
                vals[c * 16 + q : c * 16 + q + 1, :] = value[:, 0:128]
                vals[c * 16 + q + 1 : c * 16 + q + 2, :] = value[:, 128:256]

    def by_slot(rows):
        high, low = split(rows)
        both = jnp.concatenate([high, low], axis=0).astype(BF16)
        spread = dot(both, gt[...])
        count = rows.shape[0]
        spread = spread[0:count] + spread[count:]
        return [
            jnp.sum(spread[n : n + 8] * wmask[...], axis=0, keepdims=True)
            for n in range(0, count, 8)
        ]

    def put_rows(ref, base, row):
        for q in range(CAP):
            ref[base + q : base + q + 1, :] = row[:, q * 128 : (q + 1) * 128]

    def solve_wells(rate):
        spread = jnp.concatenate(
            [jnp.broadcast_to(rate[q : q + 1], (8, 128)) for q in range(CAP)], axis=1
        ) * wmask[...]
        high, low = split(spread)
        totals = dot(jnp.concatenate([high, low], axis=0).astype(BF16), gts[...])
        high, low = split(totals[0:8] + totals[8:16])
        left = jnp.concatenate(
            [
                jnp.concatenate([high, high], axis=1),
                jnp.concatenate([low, jnp.zeros_like(low)], axis=1),
            ],
            axis=0,
        ).astype(BF16)
        product = dot(left, solver[...])
        product = (product[0:8] + product[8:16]) * wmask[...]
        put_rows(mt, 0, jnp.sum(product, axis=0, keepdims=True))

    def scatter(back):
        pieces = [split(coef[3 + c] * back) for c in range(3)]
        for half in range(2):
            for q in range(CAP):
                part = slice(q * 128, (q + 1) * 128)
                into = slice((half * CAP + q) * 128, (half * CAP + q + 1) * 128)
                for c in range(3):
                    row = jnp.broadcast_to(pieces[c][half][q : q + 1], (16, 128)).astype(BF16)
                    spread = jnp.concatenate([row] * 8, axis=0)
                    terms[c * 128 : (c + 1) * 128, into] = cmb[:, part] * spread
        right = terms[...]
        left = jnp.concatenate([oht[0:128], oht[0:128]], axis=1)
        term = dot_nt(left, right)
        return [term[:, c * 128 : (c + 1) * 128] for c in range(3)]

    def couple(ref, fields, a):
        out = flat(ref[:, a, 0].astype(F32)) * fields[0]
        out = out + flat(ref[:, a, 1].astype(F32)) * fields[1]
        return out + flat(ref[:, a, 2].astype(F32)) * fields[2]

    def halo_copies(op):
        low, high = (gx + 3) % 4, (gx + 1) % 4
        left, right = (gy + 31) % 32, (gy + 1) % 32

        def row_copy(mine, theirs, which, target):
            return pltpu.make_async_remote_copy(
                src_ref=flux_pad.at[op, :, :, mine], dst_ref=flux_pad.at[op, :, :, theirs],
                send_sem=hs_sem.at[op, which], recv_sem=hr_sem.at[op, which],
                device_id=(target, gy), device_id_type=MESH,
            )

        def col_copy(which, target):
            return pltpu.make_async_remote_copy(
                src_ref=col_snd.at[op], dst_ref=col_rcv.at[op, which],
                send_sem=hs_sem.at[op, 2 + which], recv_sem=hr_sem.at[op, 2 + which],
                device_id=(gx, target), device_id_type=MESH,
            )

        return (
            row_copy(23, 7, 0, high),
            row_copy(8, 24, 1, low),
            col_copy(0, right),
            col_copy(1, left),
        )

    def stencil_start(op, fields):
        fluxes = [couple(mob_ref, fields, a) for a in range(3)]
        packed = jnp.zeros((128, 128), F32)
        for a in range(3):
            flux_pad[op, a, :, 8:24, :] = fluxes[a].reshape(8, 16, 128)
            packed = jnp.where(lane == a, fluxes[a][:, 127:128], packed)
            packed = jnp.where(lane == 3 + a, fluxes[a][:, 0:1], packed)
        col_snd[op] = packed.T[0:8]
        copies = halo_copies(op)
        for copy in copies:
            copy.start()
        centre = []
        for a in range(3):
            flux = fluxes[a]
            zero = jnp.zeros((16, 128), F32)
            out = couple(diag_ref, fields, a)
            out = out - faces[4] * jnp.concatenate([zero, flux[0:112]], axis=0)
            out = out - faces[5] * jnp.concatenate([flux[16:128], zero], axis=0)
            centre.append(out)
        return copies, centre

    def stencil_end(op, copies, centre):
        for copy in copies:
            copy.wait()
        edge_low = jnp.concatenate([col_rcv[op, 0], jnp.zeros((120, 128), F32)], axis=0).T
        edge_high = jnp.concatenate([col_rcv[op, 1], jnp.zeros((120, 128), F32)], axis=0).T
        outs = []
        for a in range(3):
            flux = flat(flux_pad[op, a, :, 8:24, :])
            before = jnp.where(lane == 0, edge_low[:, a : a + 1], pltpu.roll(flux, 1, 1))
            after = jnp.where(lane == 127, edge_high[:, 3 + a : 4 + a], pltpu.roll(flux, 127, 1))
            out = centre[a] - faces[0] * flat(flux_pad[op, a, :, 7:23, :])
            out = out - faces[1] * flat(flux_pad[op, a, :, 9:25, :])
            out = out - faces[2] * before
            outs.append(out - faces[3] * after)
        return outs

    def precondition(fields):
        paired = [field.reshape(4, 2, 16, 128) for field in fields]
        results = []
        for e in range(6):
            total = None
            for f in range(6):
                term = colinv_ref[:, e, f].astype(F32) * paired[f % 3][:, f // 3]
                total = term if total is None else total + term
            results.append(total)
        return [
            flat(jnp.concatenate([results[c][:, None], results[3 + c][:, None]], axis=1))
            for c in range(3)
        ]

    def combine(scale, xs, ys):
        return [x + scale * y for x, y in zip(xs, ys)]

    def rates_of(fields):
        gather(fields)
        return coef[0] * vals[0:16] + coef[1] * vals[16:32] + coef[2] * vals[32:48]

    def build_link():
        half = lax.bitwise_and(lax.shift_right_logical(row_of, 4), 1)
        key = lax.bitwise_and(row_of, 15) * 128 + col_of
        key = (key + lax.shift_right_logical(row_of, 5) * 2048).astype(F32)
        weights = []
        for f in range(6):
            stacked = jnp.concatenate(
                [
                    jnp.concatenate(
                        [colinv_ref[:, c, f][:, None], colinv_ref[:, 3 + c, f][:, None]], axis=1
                    ).astype(F32).reshape(128, 128).T
                    for c in range(3)
                ],
                axis=0,
            ).astype(BF16)
            for q in range(0, CAP, 2):
                part = slice(q * 128, (q + 2) * 128)
                picked = dot(stacked, oht[0:128, part])
                total = None
                for c in range(3):
                    row = jnp.concatenate(
                        [coef[c, q : q + 1, :], coef[c, q + 1 : q + 2, :]], axis=1
                    )
                    term = picked[c * 128 : (c + 1) * 128] * row
                    total = term if total is None else total + term
                total = jnp.sum(total * cmt[:, part], axis=0, keepdims=True)
                high, low = split(total)
                link_w[f : f + 1, part] = high
                link_w[6 + f : 7 + f, part] = high
                link_w[12 + f : 13 + f, part] = low
        link_w[18:32, :] = jnp.zeros((14, SLOTS), F32)
        right = link_w[...].astype(BF16)
        keys = jnp.concatenate([key[q : q + 1] for q in range(CAP)], axis=1)
        link_a[...] = jnp.zeros((128, 128), F32)
        for q in range(CAP):
            for f in range(6):
                own = jnp.where(half[q : q + 1] == f // 3, coef[3 + f % 3, q : q + 1, :], 0.0)
                high, low = split(own)
                link_a[f : f + 1, :] = high
                link_a[6 + f : 7 + f, :] = low
                link_a[12 + f : 13 + f, :] = high
            link_a[32:33, :] = key[q : q + 1]
            turned = link_a[...].T
            product = dot(turned[:, 0:32].astype(BF16), right)
            same = jnp.broadcast_to(turned[:, 32:33], (128, SLOTS)) == keys
            link[q * 128 : (q + 1) * 128, :] = jnp.where(same, product, 0.0)

    def linked(index):
        total = jnp.zeros((8, SLOTS), F32)
        for q in range(CAP):
            for n in range(0, 128, 8):
                value = jnp.broadcast_to(rcv[index, n : n + 8, q : q + 1], (8, SLOTS))
                total = total + value * link[q * 128 + n : q * 128 + n + 8, :]
        put_rows(link_out, 0, jnp.sum(total, axis=0, keepdims=True))
        return link_out[...]

    def compact_sum(left, right):
        total = jnp.sum(left * right, axis=0, keepdims=True)
        return jnp.sum(total, axis=1, keepdims=True)

    def minus_wells(applied, back):
        term = scatter(back)
        return [applied[c] - term[c] for c in range(3)]

    loads["guess"].wait()
    guess = [flat(guess_ref[:, c]) for c in range(3)]
    gather(guess)
    for c in range(3):
        mt[CAP * c : CAP * (c + 1), :] = vals[16 * c : 16 * c + CAP]
    loads["slot"].wait()
    slots = slot_ref[:, 0, :]
    well_of = lax.shift_right_logical(slots, 7)
    seg_of = lax.bitwise_and(slots, 127)
    for q in range(CAP):
        part = slice(q * 128, (q + 1) * 128)
        seg_hot = jnp.where(sub == seg_of[q : q + 1], 1.0, 0.0)
        gt[:, part] = seg_hot.astype(BF16)
        gts[part, :] = seg_hot.T.astype(BF16)
        wmask[:, part] = jnp.where(sub8 == well_of[q : q + 1], 1.0, 0.0)
    for name in ("win", "wout"):
        loads[name].wait()
    rows = [ref[c : c + 1, w * 128 : (w + 1) * 128] for ref in (win_ref, wout_ref) for c in range(3) for w in range(8)]
    own = by_slot(jnp.concatenate(rows, axis=0))
    for n in range(6):
        put_rows(mt, (3 + n) * CAP, own[n])
    for c in range(3):
        put_rows(own_in, c * 16, own[c])
    snd[0] = mt[...].T
    pl.semaphore_wait(barrier, DEV - 1)
    send(0)
    for name in ("mob", "diag", "right", "colinv"):
        loads[name].wait()
    inner = lax.bitwise_and(sub, 15)
    layer = lax.shift_right_logical(sub, 4)
    outside = (
        (inner == 0) & (gx == 0),
        (inner == 15) & (gx == 3),
        (lane == 0) & (gy == 0),
        (lane == 127) & (gy == 31),
        layer == 0,
        layer == 7,
    )
    loads["face"].wait()
    for n in range(6):
        faces[n] = jnp.where(outside[n], 0.0, flat(face_ref[n].astype(F32)))

    started = stencil_start(0, guess)
    loads["winv"].wait()
    fused = None
    for w in range(8):
        high, low = split(winv_ref[w].T)
        rows = dot(high.astype(BF16), gt[...]) + dot(low.astype(BF16), gt[...])
        rows = rows * wmask[w : w + 1, :]
        fused = rows if fused is None else fused + rows
    high, low = split(fused)
    solver[0:128, :] = high.astype(BF16)
    solver[128:256, :] = low.astype(BF16)

    coef[...] = jnp.zeros((6, 16, 128), F32)
    link_out[...] = jnp.zeros((16, 128), F32)
    got = receive(0)
    mt[...] = jnp.zeros((128, 128), F32)
    solve_wells(sum(own_in[16 * c : 16 * c + CAP, :] * got[CAP * c : CAP * (c + 1)] for c in range(3)))
    post(1)
    for n in range(6):
        coef[n, 0:CAP, :] = got[(3 + n) * CAP : (4 + n) * CAP]

    applied = stencil_end(0, *started)
    part0 = [flat(right_ref[:, c]) - applied[c] for c in range(3)]
    rates_d = rates_of(precondition(part0))
    build_link()
    got = receive(1)
    mt[0:16, :] = rates_d + linked(1)
    post(2)
    term = scatter(got[0:16])
    r0 = [part0[c] + term[c] for c in range(3)]
    u1 = precondition(r0)
    started = stencil_start(1, u1)
    gather(r0)
    r0_out = coef[3] * vals[0:16] + coef[4] * vals[16:32] + coef[5] * vals[32:48]
    own_rho = local_sum(r0, r0)
    solve_wells(receive(2)[0:16])
    post(3, [own_rho])
    d1 = stencil_end(1, *started)
    rates_d = rates_of(precondition(d1))
    own_d = local_sum(r0, d1)
    got = receive(3)
    rho0 = lane_sum(got, 0)
    back = got[0:16]
    rates2 = rates_d - linked(3)
    own_v = own_d - compact_sum(r0_out, back)
    mt[0:16, :] = rates2
    post(4, [own_v])
    v0 = minus_wells(d1, back)
    u2 = precondition(v0)
    started = stencil_start(2, u2)
    got = receive(4)
    alpha0 = rho0 / lane_sum(got, 0)
    solve_wells(got[0:16])
    post(5)
    d2 = stencil_end(2, *started)
    rates_d = rates_of(precondition(d2))
    got = receive(5)
    rates_y = rates_d - linked(5)
    rates3 = rates2 - alpha0 * rates_y
    mt[0:16, :] = rates3
    post(6)
    y0 = minus_wells(d2, got[0:16])
    s0 = combine(-alpha0, r0, v0)
    t0 = combine(-alpha0, v0, y0)
    u3 = precondition(t0)
    started = stencil_start(3, u3)
    own_y = local_sum(r0, y0)
    own_t = local_sum(r0, t0)
    own_dots = [local_sum(t0, s0), local_sum(t0, t0), local_sum(r0, s0), own_t]
    solve_wells(receive(6)[0:16])
    post(7, own_dots)
    d3 = stencil_end(3, *started)
    rates_d = rates_of(precondition(d3))
    own_d = local_sum(r0, d3)
    got = receive(7)
    omega0 = lane_sum(got, 0) / lane_sum(got, 1)
    rho1 = lane_sum(got, 2) - omega0 * lane_sum(got, 3)
    beta = rho1 / rho0 * (alpha0 / omega0)
    back = got[0:16]
    rates_w = rates_d - linked(7)
    mt[0:16, :] = rates3 - omega0 * rates_w + beta * (rates2 - omega0 * rates_y)
    own_w = own_d - compact_sum(r0_out, back)
    post(8, [own_t - omega0 * own_w + beta * (own_v - omega0 * own_y)])
    w0 = minus_wells(d3, back)
    r1 = combine(-omega0, s0, t0)
    a_r1 = combine(-omega0, t0, w0)
    v1 = combine(beta, a_r1, combine(-omega0, v0, y0))
    u4 = precondition(v1)
    started = stencil_start(4, u4)
    got = receive(8)
    alpha1 = rho1 / lane_sum(got, 0)
    solve_wells(got[0:16])
    post(9)
    d4 = stencil_end(4, *started)
    s1 = combine(-alpha1, r1, v1)
    got = receive(9)
    t1 = combine(-alpha1, a_r1, minus_wells(d4, got[0:16]))
    snd[10] = jnp.where(lane == 16, local_sum(t1, s1), jnp.where(lane == 17, local_sum(t1, t1), 0.0))
    send(10)
    ms0 = combine(-alpha0, u1, u2)
    mr1 = combine(-omega0, ms0, u3)
    mp1 = combine(beta, mr1, combine(-omega0, u1, u2))
    ms1 = combine(-alpha1, mr1, u4)
    guess = [flat(guess_ref[:, c]) for c in range(3)]
    partial = combine(alpha1, combine(omega0, combine(alpha0, guess, u1), ms0), mp1)
    for index in range(EXCHANGES - 1):
        sent(index)
    arrive(10)
    sums = jnp.sum(rcv[10], axis=0, keepdims=True)
    omega1 = sums[:, 16:17] / sums[:, 17:18]
    final = combine(omega1, partial, ms1)
    left = combine(-omega1, s1, t1)
    for c in range(3):
        sol_ref[:, c] = final[c].reshape(8, 16, 128)
        res_ref[:, c] = left[c].reshape(8, 16, 128)
    sent(10)


def per_device(*args):
    args = list(args)
    for n in (6, 7):
        args[n] = jnp.transpose(args[n], (2, 0, 1))
    shape = args[0].shape
    hbm = pl.BlockSpec(memory_space=pltpu.HBM)
    vmem = pl.BlockSpec(memory_space=pltpu.VMEM)
    return pl.pallas_call(
        kernel,
        out_shape=(jax.ShapeDtypeStruct(shape, F32), jax.ShapeDtypeStruct(shape, F32)),
        in_specs=[hbm] * 11,
        out_specs=(vmem, vmem),
        scratch_shapes=[pltpu.VMEM(arg.shape, arg.dtype) for arg in args]
        + [
            pltpu.SemaphoreType.DMA((11,)),
            pltpu.VMEM((EXCHANGES, 128, 128), F32),
            pltpu.VMEM((EXCHANGES, 128, 128), F32),
            pltpu.VMEM((OPS, 3, 8, 32, 128), F32),
            pltpu.VMEM((OPS, 8, 128), F32),
            pltpu.VMEM((OPS, 2, 8, 128), F32),
            pltpu.VMEM((128, 128), F32),
            pltpu.VMEM((6, 128, 128), F32),
            pltpu.VMEM((256, SLOTS), BF16),
            pltpu.VMEM((128, SLOTS), F32),
            pltpu.VMEM((128, SLOTS), BF16),
            pltpu.VMEM((384, 2 * SLOTS), BF16),
            pltpu.VMEM((SLOTS, 128), BF16),
            pltpu.VMEM((128, SLOTS), BF16),
            pltpu.VMEM((8, SLOTS), F32),
            pltpu.VMEM((256, SLOTS), BF16),
            pltpu.VMEM((48, 128), F32),
            pltpu.VMEM((6, 16, 128), F32),
            pltpu.VMEM((SLOTS, SLOTS), F32),
            pltpu.VMEM((32, SLOTS), F32),
            pltpu.VMEM((128, 128), F32),
            pltpu.VMEM((16, 128), F32),
            pltpu.VMEM((48, 128), F32),
            pltpu.SemaphoreType.DMA((EXCHANGES,)),
            pltpu.SemaphoreType.DMA((EXCHANGES,)),
            pltpu.SemaphoreType.DMA((OPS, 4)),
            pltpu.SemaphoreType.DMA((OPS, 4)),
        ],
        compiler_params=pltpu.CompilerParams(
            collective_id=0, has_side_effects=True, vmem_limit_bytes=60 * 1024 * 1024
        ),
    )(*args)


def solution(mesh):
    in_specs = (
        P(None, None, "gx", "gy"),
        P(None, None, "gx", "gy"),
        P(None, None, None, "gx", "gy"),
        P(None, None, None, "gx", "gy"),
        P(None, None, "gx", "gy"),
        P(None, None, None, "gx", "gy"),
        P(("gx", "gy"), None, None),
        P(("gx", "gy"), None, None),
        P(None, ("gx", "gy")),
        P(None, ("gx", "gy")),
        P(("gx", "gy"), None, None),
    )
    out_specs = (P(None, None, "gx", "gy"), P(None, None, "gx", "gy"))
    return jax.shard_map(
        per_device, mesh=mesh, in_specs=in_specs, out_specs=out_specs, check_vma=False
    )
```
